256 devices in a mesh: gx: 8 (over z), gz: 8 (over x, core), gy: 4 (over y).
Axes of the slice: x: 4, y: 4, z: 8, core: 2. Of those that a mesh axis runs over, the one named last changes fastest.
Arguments:
- velocity: float32 [3, 512, 512, 512], P(None, ('gx', 'gz'), None, 'gy'), may hold values from -5 to 5, as said below
- spacing: float32 [513], replicated, may hold values from 0.15 to 3.4, as said below
Outputs:
- pressure: float32 [512, 512, 512], P(('gx', 'gz'), None, 'gy')
The draws below stay inside these ranges and needn't reach their ends.
Inputs may be any that keep to these rules, and one draw needn't show every extreme that they name: `velocity`: velocity components at the grid nodes. `spacing`: entry 0 is the gap from the lower wall to the first node and entry 512 the gap from the last node to the upper wall.
All inputs are finite; a program needn't handle non-finite values.
Results may differ from the reference program's by a relative error of at most 0.0003.
Values sent between devices are 32-bit elements; how exact they have to be, the bound alone decides.
No kernel may reach another device: no remote copies, remote signals or barrier semaphores. Data moves between devices by JAX's collectives and lax.ppermute only.
A program may use at most 64 MiB of HBM per device.

```python
import math
import jax
import jax.numpy as jnp
from jax import lax

NX = 512
NY = 512
NZ = 512


def draw_velocity(key, part):
    values = jnp.clip(jax.random.normal(key, (3, NZ, NX, NY), jnp.float32), -5.0, 5.0)
    return values


def draw_spacing(key, part):
    index = jnp.arange(NY + 1, dtype=jnp.float32)
    profile = 1.0 - 0.7 * jnp.cos(2.0 * math.pi * (index + 0.5) / (NY + 1))
    factor = jnp.exp(jax.random.uniform(key, (NY + 1,), jnp.float32, math.log(0.6), math.log(1.5)))
    return profile * factor


def setup_inputs(seed: int = 0) -> dict:
    splits = jax.random.split(jax.random.key(seed), 3)
    velocity = draw_velocity(jax.random.fold_in(splits[2], 71), 0)
    spacing = draw_spacing(jax.random.fold_in(splits[2], 71), 0)
    return dict(velocity=velocity, spacing=spacing)


span_step = 0.5


def wave_numbers(length, step_size):
    index = jnp.arange(length)
    wave = jnp.where(index == 1, length // 2, index // 2)
    return (2.0 * math.pi / (length * step_size)) * wave.astype(jnp.float32)


def to_modes(field, axis):
    moved = jnp.moveaxis(field, axis, -1)
    length = moved.shape[-1]
    half = length // 2
    spectrum = jnp.fft.rfft(moved, axis=-1)
    real_part = jnp.real(spectrum)[..., :half]
    imag_part = jnp.concatenate([jnp.real(spectrum)[..., half:half + 1], jnp.imag(spectrum)[..., 1:half]], axis=-1)
    packed = jnp.stack([real_part, imag_part], axis=-1).reshape(moved.shape)
    return jnp.moveaxis(packed, -1, axis)


def from_modes(packed, axis):
    moved = jnp.moveaxis(packed, axis, -1)
    length = moved.shape[-1]
    real_part = moved[..., 0::2]
    imag_part = moved[..., 1::2]
    zeros = jnp.zeros_like(real_part[..., :1])
    spectrum_real = jnp.concatenate([real_part, imag_part[..., :1]], axis=-1)
    spectrum_imag = jnp.concatenate([zeros, imag_part[..., 1:], zeros], axis=-1)
    values = jnp.fft.irfft(spectrum_real + 1j * spectrum_imag, n=length, axis=-1)
    return jnp.moveaxis(values, -1, axis)


def derivative(packed, axis, step_size):
    moved = jnp.moveaxis(packed, axis, -1)
    length = moved.shape[-1]
    half = length // 2
    kappa = (2.0 * math.pi / (length * step_size)) * jnp.arange(half).astype(jnp.float32)
    real_part = moved[..., 0::2]
    imag_part = moved[..., 1::2]
    result = jnp.stack([-kappa * imag_part, kappa * real_part], axis=-1).reshape(moved.shape)
    return jnp.moveaxis(result, -1, axis)


def reference(velocity, spacing):
    width = spacing[:-1] + spacing[1:]
    lower = 2.0 / (width * spacing[:-1])
    upper = 2.0 / (width * spacing[1:])
    padded = jnp.pad(velocity[1], ((0, 0), (0, 0), (1, 1)))
    normal_slope = (padded[..., 2:] - padded[..., :-2]) / width
    flow_part = derivative(to_modes(velocity[0], 1), 1, 1.0) + to_modes(normal_slope, 1)
    span_part = to_modes(velocity[2], 1)
    source = to_modes(flow_part, 0) + derivative(to_modes(span_part, 0), 0, span_step)
    sigma = wave_numbers(NZ, span_step)[:, None] ** 2 + wave_numbers(NX, 1.0)[None, :] ** 2
    diagonal = -(lower + upper)
    lower_row = lower.at[0].set(0.0)
    upper_row = upper.at[-1].set(0.0)

    def solve_block(pair):
        block, sigma_block = pair
        start = jnp.zeros(sigma_block.shape, jnp.float32)

        def forward(carry, row):
            ratio, value = carry
            side, lower_value, diagonal_value, upper_value = row
            pivot = diagonal_value - sigma_block - lower_value * ratio
            ratio_next = upper_value / pivot
            value_next = (side - lower_value * value) / pivot
            return (ratio_next, value_next), (ratio_next, value_next)

        rows_first = jnp.moveaxis(block, -1, 0)
        unused, (ratios, values) = lax.scan(forward, (start, start), (rows_first, lower_row, diagonal, upper_row))

        def backward(after, row):
            ratio, value = row
            current = value - ratio * after
            return current, current

        unused, solved = lax.scan(backward, start, (ratios, values), reverse=True)
        return jnp.moveaxis(solved, 0, -1)

    blocks = 8
    modes = lax.map(solve_block, (source.reshape(blocks, NZ // blocks, NX, NY), sigma.reshape(blocks, NZ // blocks, NX)))
    modes = modes.reshape(NZ, NX, NY)
    return from_modes(from_modes(modes, 0), 1)
```

```python
import functools
import math

import jax
import jax.numpy as jnp
import ml_dtypes
import numpy as np
from jax import lax
from jax.experimental import pallas as pl
from jax.experimental.pallas import tpu as pltpu
from jax.sharding import PartitionSpec as P

span_step = 0.5
f32 = jnp.float32
bf16 = jnp.bfloat16


def np_tables(length, step_size):
    index = np.arange(length)
    wave = np.where(index == 1, length // 2, index // 2)
    phase = (index[:, None] * wave[None, :]) % length
    angle = 2.0 * math.pi / length * phase
    odd_high = np.logical_and(index % 2 == 1, index >= 3)[None, :]
    forward = np.where(odd_high, -np.sin(angle), np.cos(angle))
    kappa = 2.0 * math.pi / (length * step_size) * wave
    scale = np.where(index >= 2, kappa, 0.0)[None, :]
    derive = np.where(odd_high, np.cos(angle), np.sin(angle)) * scale
    weight = np.where(index >= 2, 2.0, 1.0) / length
    inverse = (forward * weight[None, :]).T
    return forward, derive, inverse, (kappa * kappa).astype(np.float32)


def split_np(table):
    high = table.astype(np.float32).astype(ml_dtypes.bfloat16)
    low = (table - high.astype(np.float64)).astype(np.float32).astype(ml_dtypes.bfloat16)
    return high, low


def left_table(table):
    high, low = split_np(table)
    return np.concatenate([high, low, high], axis=1)


def right_table(table):
    high, low = split_np(table)
    return np.concatenate([high, low, high], axis=0)


def parts(x, axis):
    high = x.astype(bf16)
    low = (x - high.astype(f32)).astype(bf16)
    return jnp.concatenate([high, high, low], axis=axis)


def params(mib):
    return pltpu.CompilerParams(vmem_limit_bytes=mib * 1024 * 1024)


def cost(flops, size):
    return pl.CostEstimate(flops=flops, bytes_accessed=size, transcendentals=0)


def span_field_kernel(w_ref, t_ref, o_ref):
    x = jnp.concatenate([w_ref[0, 0], w_ref[0, 1]], axis=1)
    y = jnp.dot(t_ref[...], parts(x, 0), preferred_element_type=f32)
    for p in range(2):
        part = y[:, 128 * p : 128 * (p + 1)]
        o_ref[:, p] = part.reshape(part.shape[0] // 8, 8, 128)


def flow_field_kernel(u_ref, v_ref, before_ref, after_ref, width_ref, t_ref, o_ref):
    step = pl.program_id(0)
    lane = lax.broadcasted_iota(jnp.int32, v_ref.shape[2:], 1)
    width = width_ref[...]
    slopes = []
    for p in range(2):
        v = v_ref[0, p]
        z = step * 2 + p
        before = jnp.transpose(jnp.broadcast_to(before_ref[pl.ds(z, 1), :], (128, v.shape[0])))
        after = jnp.transpose(jnp.broadcast_to(after_ref[pl.ds(z, 1), :], (128, v.shape[0])))
        down = jnp.where(lane == 0, before, pltpu.roll(v, 1, 1))
        up = jnp.where(lane == 127, after, pltpu.roll(v, 127, 1))
        slopes.append((up - down) / width)
    u = jnp.concatenate([u_ref[0, 0], u_ref[0, 1]], axis=1)
    s = jnp.concatenate(slopes, axis=1)
    x = jnp.concatenate([parts(u, 0), parts(s, 0)], axis=0)
    y = jnp.dot(t_ref[...], x, preferred_element_type=f32)
    for p in range(2):
        part = y[:, 128 * p : 128 * (p + 1)]
        o_ref[:, p] = part.reshape(part.shape[0] // 8, 8, 128)


def factor_kernel(low_ref, up_ref, sigma_ref, inv_ref, m_ref, r_ref, v_ref, w_ref, ends_ref):
    rows = inv_ref.shape[0]
    tiles = inv_ref.shape[1]

    def ahead(y, carry):
        low = low_ref[y]
        up = up_ref[y]
        out = []
        for t in range(tiles):
            r, val = carry[t]
            pivot = -(low + up) - sigma_ref[t] - low * r
            inv = 1.0 / pivot
            r = up * inv
            m = low * inv
            val = -m * val
            inv_ref[y, t] = inv
            m_ref[y, t] = m
            r_ref[y, t] = r
            v_ref[t, pl.ds(y, 8, stride=rows), :] = val
            out.append((r, val))
        return tuple(out)

    zero = jnp.zeros((8, 128), f32)
    one = jnp.ones((8, 128), f32)
    lax.fori_loop(0, rows, ahead, ((zero, one),) * tiles)

    def back(s, carry):
        y = rows - 1 - s
        out = []
        for t in range(tiles):
            v, w = carry[t]
            r = r_ref[y, t]
            v = v_ref[t, pl.ds(y, 8, stride=rows), :] - r * v
            w = -r * w
            v_ref[t, pl.ds(y, 8, stride=rows), :] = v
            w_ref[t, pl.ds(y, 8, stride=rows), :] = w
            out.append((v, w))
        return tuple(out)

    first = lax.fori_loop(0, rows, back, ((zero, one),) * tiles)
    for t in range(tiles):
        ends_ref[0, t] = first[t][0]
        ends_ref[1, t] = v_ref[t, pl.ds(rows - 1, 8, stride=rows), :]
        ends_ref[2, t] = first[t][1]
        ends_ref[3, t] = w_ref[t, pl.ds(rows - 1, 8, stride=rows), :]


def span_modes(x_ref, t_ref, mode):
    planes = x_ref.shape[0] // 8
    both = [
        jnp.transpose(x_ref[pl.ds(mode + p, planes, stride=8), :]) for p in range(2)
    ]
    x = jnp.concatenate(both, axis=0)
    return jnp.dot(parts(x, 1), t_ref[...], preferred_element_type=f32)


def span_first_kernel(x_ref, t_ref, o_ref):
    tiles = o_ref.shape[0]
    for mode in range(0, 8, 2):
        y = span_modes(x_ref, t_ref, mode)
        for t in range(tiles):
            o_ref[t, mode * 128 : (mode + 2) * 128, :] = y[:, t * 128 : (t + 1) * 128]


def sweep_kernel(x_ref, s_ref, t_ref, inv_ref, m_ref, r_ref, o_ref, ends_ref):
    tiles = o_ref.shape[0]
    rows = inv_ref.shape[0]
    for mode in range(0, 8, 2):
        y = span_modes(x_ref, t_ref, mode)
        part = slice(mode * 128, (mode + 2) * 128)
        for t in range(tiles):
            o_ref[t, part, :] = y[:, t * 128 : (t + 1) * 128] + s_ref[t, part, :]

    def ahead(y, carry):
        out = []
        for t in range(tiles):
            side = o_ref[t, pl.ds(y, 8, stride=rows), :]
            val = side * inv_ref[y, t] - m_ref[y, t] * carry[t]
            o_ref[t, pl.ds(y, 8, stride=rows), :] = val
            out.append(val)
        return tuple(out)

    zero = jnp.zeros((8, 128), f32)
    lax.fori_loop(0, rows, ahead, (zero,) * tiles, unroll=4)

    def back(s, carry):
        y = rows - 1 - s
        out = []
        for t in range(tiles):
            val = o_ref[t, pl.ds(y, 8, stride=rows), :] - r_ref[y, t] * carry[t]
            o_ref[t, pl.ds(y, 8, stride=rows), :] = val
            out.append(val)
        return tuple(out)

    first = lax.fori_loop(0, rows, back, (zero,) * tiles, unroll=4)
    for t in range(tiles):
        ends_ref[0, t] = first[t]
        ends_ref[1, t] = o_ref[t, pl.ds(rows - 1, 8, stride=rows), :]


def join_kernel(me_ref, y_ref, v_ref, w_ref, ys_ref, vw_ref, t_ref, o_ref, b_ref, f_ref):
    blocks = vw_ref.shape[0]
    tiles = y_ref.shape[0]
    me = me_ref[0]
    for t in range(tiles):
        alpha = jnp.zeros((8, 128), f32)
        beta = jnp.zeros((8, 128), f32)
        alphas, betas, starts, scales = [], [], [], []
        for g in range(blocks):
            slot = lax.rem(me + blocks - g, blocks)
            yf = ys_ref[slot, 0, t]
            yb = ys_ref[slot, 1, t]
            vf, vb, wf, wb = (vw_ref[g, n, t] for n in range(4))
            scale = 1.0 / (1.0 - vf * beta)
            start = (yf + vf * alpha) * scale
            starts.append(start)
            scales.append(wf * scale)
            alpha, beta = (
                yb + vb * (alpha + beta * start),
                wb + vb * beta * wf * scale,
            )
            alphas.append(alpha)
            betas.append(beta)
        after = jnp.zeros((8, 128), f32)
        f_ref[blocks, t] = after
        b_ref[0, t] = after
        for g in range(blocks - 1, -1, -1):
            b_ref[g + 1, t] = alphas[g] + betas[g] * after
            after = starts[g] + scales[g] * after
            f_ref[g, t] = after
    for mode in range(0, 8, 2):
        columns = []
        for t in range(tiles):
            both = []
            for p in range(2):
                part = slice((mode + p) * 128, (mode + p + 1) * 128)
                left = b_ref[me, t, pl.ds(mode + p, 1), :]
                right = f_ref[me + 1, t, pl.ds(mode + p, 1), :]
                both.append(y_ref[t, part, :] + v_ref[t, part, :] * left + w_ref[t, part, :] * right)
            columns.append(jnp.concatenate(both, axis=0))
        x = jnp.concatenate(columns, axis=1)
        y = lax.dot_general(
            t_ref[...], parts(x, 1), (((1,), (1,)), ((), ())), preferred_element_type=f32
        )
        for p in range(2):
            part = y[:, 128 * p : 128 * (p + 1)]
            o_ref[:, mode + p] = part.reshape(part.shape[0] // 8, 8, 128)


def flow_inverse_kernel(x_ref, t_ref, o_ref):
    slots = x_ref.shape[0] // 8
    for plane in range(0, 8, 2):
        x = jnp.concatenate(
            [x_ref[pl.ds(plane + p, slots, stride=8), :] for p in range(2)], axis=1
        )
        y = jnp.dot(t_ref[...], parts(x, 0), preferred_element_type=f32)
        for p in range(2):
            o_ref[plane + p] = y[:, 128 * p : 128 * (p + 1)]


def local(velocity, spacing):
    planes, flow_length, rows = velocity.shape[1:]
    size_x = lax.axis_size("gx")
    size_z = lax.axis_size("gz")
    blocks = lax.axis_size("gy")
    group = size_x * size_z
    span_length = planes * group
    modes = flow_length // group
    tiles = span_length // 128
    flow_forward, flow_derive, flow_inverse, flow_square = np_tables(flow_length, 1.0)
    span_forward, span_derive, span_inverse, span_square = np_tables(span_length, span_step)
    field_flops = 2 * 3 * planes * rows * flow_length * flow_length
    field_bytes = 4 * planes * rows * flow_length
    me = lax.axis_index("gy")
    both = ("gx", "gz")

    def moved(x):
        return lax.all_to_all(x, both, split_axis=0, concat_axis=0, tiled=True)

    field_shape = jax.ShapeDtypeStruct((group, planes, modes, rows), f32)
    table = jnp.asarray(left_table(flow_forward.T))
    plane_block = lambda c: pl.BlockSpec((1, 2, flow_length, rows), lambda i: (c, i, 0, 0))
    whole = lambda *shape: pl.BlockSpec(shape, lambda i: (0,) * len(shape))
    out_block = pl.BlockSpec((group, 2, modes, rows), lambda i: (0, i, 0, 0))
    span_sent = pl.pallas_call(
        span_field_kernel,
        grid=(planes // 2,),
        in_specs=[plane_block(2), whole(*table.shape)],
        out_specs=out_block,
        out_shape=field_shape,
        compiler_params=params(32),
        cost_estimate=cost(field_flops, 2 * field_bytes),
        name="span_field",
    )(velocity, table)
    span_here = moved(span_sent)

    v = velocity[1]
    up = [(i, i + 1) for i in range(blocks - 1)]
    down = [(j, i) for i, j in up]
    before = lax.ppermute(v[:, :, rows - 1], "gy", up)
    after = lax.ppermute(v[:, :, 0], "gy", down)
    gaps = lax.dynamic_slice_in_dim(spacing, me * rows, rows + 1)
    width = gaps[:-1] + gaps[1:]
    lower = 2.0 / (width * gaps[:-1])
    upper = 2.0 / (width * gaps[1:])
    flow_table = jnp.asarray(
        np.concatenate([left_table(flow_derive.T), left_table(flow_forward.T)], axis=1)
    )
    flow_sent = pl.pallas_call(
        flow_field_kernel,
        grid=(planes // 2,),
        in_specs=[
            plane_block(0),
            plane_block(1),
            whole(planes, flow_length),
            whole(planes, flow_length),
            whole(1, rows),
            whole(*flow_table.shape),
        ],
        out_specs=out_block,
        out_shape=field_shape,
        compiler_params=params(40),
        cost_estimate=cost(2 * field_flops, 3 * field_bytes),
        name="flow_field",
    )(velocity, velocity, before, after, width.reshape(1, rows), flow_table)
    flow_here = moved(flow_sent)

    first_mode = (lax.axis_index("gx") * size_z + lax.axis_index("gz")) * modes
    mode_square = lax.dynamic_slice_in_dim(jnp.asarray(flow_square), first_mode, modes)
    sigma = mode_square[None, :, None] + jnp.asarray(span_square).reshape(tiles, 1, 128)
    step_shape = jax.ShapeDtypeStruct((rows, tiles, modes, 128), f32)
    slab_shape = jax.ShapeDtypeStruct((tiles, modes * rows, 128), f32)
    vmem = pl.BlockSpec(memory_space=pltpu.VMEM)
    smem = pl.BlockSpec(memory_space=pltpu.SMEM)
    inv, m, r, v_all, w_all, vw_ends = pl.pallas_call(
        factor_kernel,
        in_specs=[smem, smem, vmem],
        out_specs=[vmem] * 6,
        out_shape=[step_shape] * 3
        + [slab_shape] * 2
        + [jax.ShapeDtypeStruct((4, tiles, modes, 128), f32)],
        compiler_params=params(32),
        cost_estimate=cost(field_flops, 5 * field_bytes),
        name="factor",
    )(lower, upper, sigma)
    vw = lax.all_gather(vw_ends, "gy", axis=0, tiled=False)

    flat = (span_length * modes, rows)
    span_source = pl.pallas_call(
        span_first_kernel,
        in_specs=[vmem, vmem],
        out_specs=vmem,
        out_shape=slab_shape,
        compiler_params=params(32),
        cost_estimate=cost(field_flops, 2 * field_bytes),
        name="span_first",
    )(span_here.reshape(flat), jnp.asarray(right_table(span_derive)))
    y_all, y_ends = pl.pallas_call(
        sweep_kernel,
        in_specs=[vmem] * 6,
        out_specs=[vmem] * 2,
        out_shape=[slab_shape, jax.ShapeDtypeStruct((2, tiles, modes, 128), f32)],
        compiler_params=params(40),
        cost_estimate=cost(field_flops, 6 * field_bytes),
        name="sweep",
    )(flow_here.reshape(flat), span_source, jnp.asarray(right_table(span_forward)), inv, m, r)
    shifted = [y_ends] + [
        lax.ppermute(y_ends, "gy", [(i, (i + s) % blocks) for i in range(blocks)])
        for s in range(1, blocks)
    ]
    ys = jnp.stack(shifted)
    end_shape = (blocks + 1, tiles, modes, 128)
    back_sent = pl.pallas_call(
        join_kernel,
        in_specs=[smem] + [vmem] * 6,
        out_specs=vmem,
        out_shape=jax.ShapeDtypeStruct((group, modes, planes, rows), f32),
        scratch_shapes=[pltpu.VMEM(end_shape, f32), pltpu.VMEM(end_shape, f32)],
        compiler_params=params(40),
        cost_estimate=cost(field_flops, 4 * field_bytes),
        name="join",
    )(
        me.reshape(1).astype(jnp.int32),
        y_all,
        v_all,
        w_all,
        ys,
        vw,
        jnp.asarray(left_table(span_inverse.T)),
    )
    back_here = moved(back_sent)
    return pl.pallas_call(
        flow_inverse_kernel,
        in_specs=[vmem, vmem],
        out_specs=vmem,
        out_shape=jax.ShapeDtypeStruct((planes, flow_length, rows), f32),
        compiler_params=params(32),
        cost_estimate=cost(field_flops, 2 * field_bytes),
        name="flow_inverse",
    )(back_here.reshape(flow_length * planes, rows), jnp.asarray(left_table(flow_inverse.T)))


def solution(mesh):
    return jax.shard_map(
        local,
        mesh=mesh,
        in_specs=(P(None, ("gx", "gz"), None, "gy"), P()),
        out_specs=P(("gx", "gz"), None, "gy"),
        check_vma=False,
    )
```

```python
import functools
import math

import jax
import jax.numpy as jnp
import ml_dtypes
import numpy as np
from jax import lax
from jax.experimental import pallas as pl
from jax.experimental.pallas import tpu as pltpu
from jax.sharding import PartitionSpec as P

span_step = 0.5
f32 = jnp.float32
bf16 = jnp.bfloat16


def np_tables(length, step_size):
    index = np.arange(length)
    wave = np.where(index == 1, length // 2, index // 2)
    phase = (index[:, None] * wave[None, :]) % length
    angle = 2.0 * math.pi / length * phase
    odd_high = np.logical_and(index % 2 == 1, index >= 3)[None, :]
    forward = np.where(odd_high, -np.sin(angle), np.cos(angle))
    kappa = 2.0 * math.pi / (length * step_size) * wave
    scale = np.where(index >= 2, kappa, 0.0)[None, :]
    derive = np.where(odd_high, np.cos(angle), np.sin(angle)) * scale
    weight = np.where(index >= 2, 2.0, 1.0) / length
    inverse = (forward * weight[None, :]).T
    return forward, derive, inverse, (kappa * kappa).astype(np.float32)


def split_np(table):
    high = table.astype(np.float32).astype(ml_dtypes.bfloat16)
    low = (table - high.astype(np.float64)).astype(np.float32).astype(ml_dtypes.bfloat16)
    return high, low


def left_table(table):
    high, low = split_np(table)
    return np.concatenate([high, low, high], axis=1)


def right_table(table):
    high, low = split_np(table)
    return np.concatenate([high, low, high], axis=0)


def parts(x, axis):
    high = x.astype(bf16)
    low = (x - high.astype(f32)).astype(bf16)
    return jnp.concatenate([high, high, low], axis=axis)


def params(mib):
    return pltpu.CompilerParams(vmem_limit_bytes=mib * 1024 * 1024)


def cost(flops, size):
    return pl.CostEstimate(flops=flops, bytes_accessed=size, transcendentals=0)


def span_field_kernel(w_ref, t_ref, o_ref):
    x = jnp.concatenate([w_ref[0, 0], w_ref[0, 1]], axis=1)
    y = jnp.dot(t_ref[...], parts(x, 0), preferred_element_type=f32)
    for p in range(2):
        part = y[:, 128 * p : 128 * (p + 1)]
        o_ref[:, p] = part.reshape(part.shape[0] // 8, 8, 128)


def flow_field_kernel(u_ref, v_ref, before_ref, after_ref, width_ref, t_ref, o_ref):
    step = pl.program_id(0)
    lane = lax.broadcasted_iota(jnp.int32, v_ref.shape[2:], 1)
    width = width_ref[...]
    slopes = []
    for p in range(2):
        v = v_ref[0, p]
        z = step * 2 + p
        before = jnp.transpose(jnp.broadcast_to(before_ref[pl.ds(z, 1), :], (128, v.shape[0])))
        after = jnp.transpose(jnp.broadcast_to(after_ref[pl.ds(z, 1), :], (128, v.shape[0])))
        down = jnp.where(lane == 0, before, pltpu.roll(v, 1, 1))
        up = jnp.where(lane == 127, after, pltpu.roll(v, 127, 1))
        slopes.append((up - down) / width)
    u = jnp.concatenate([u_ref[0, 0], u_ref[0, 1]], axis=1)
    s = jnp.concatenate(slopes, axis=1)
    x = jnp.concatenate([parts(u, 0), parts(s, 0)], axis=0)
    y = jnp.dot(t_ref[...], x, preferred_element_type=f32)
    for p in range(2):
        part = y[:, 128 * p : 128 * (p + 1)]
        o_ref[:, p] = part.reshape(part.shape[0] // 8, 8, 128)


def factor_kernel(low_ref, up_ref, sigma_ref, inv_ref, m_ref, r_ref, v_ref, w_ref, ends_ref):
    rows = inv_ref.shape[0]
    tiles = inv_ref.shape[1]

    def ahead(y, carry):
        low = low_ref[y]
        up = up_ref[y]
        out = []
        for t in range(tiles):
            r, val = carry[t]
            pivot = -(low + up) - sigma_ref[t] - low * r
            inv = 1.0 / pivot
            r = up * inv
            m = low * inv
            val = -m * val
            inv_ref[y, t] = inv
            m_ref[y, t] = m
            r_ref[y, t] = r
            v_ref[t, pl.ds(y, 8, stride=rows), :] = val
            out.append((r, val))
        return tuple(out)

    zero = jnp.zeros((8, 128), f32)
    one = jnp.ones((8, 128), f32)
    lax.fori_loop(0, rows, ahead, ((zero, one),) * tiles)

    def back(s, carry):
        y = rows - 1 - s
        out = []
        for t in range(tiles):
            v, w = carry[t]
            r = r_ref[y, t]
            v = v_ref[t, pl.ds(y, 8, stride=rows), :] - r * v
            w = -r * w
            v_ref[t, pl.ds(y, 8, stride=rows), :] = v
            w_ref[t, pl.ds(y, 8, stride=rows), :] = w
            out.append((v, w))
        return tuple(out)

    first = lax.fori_loop(0, rows, back, ((zero, one),) * tiles)
    for t in range(tiles):
        ends_ref[0, t] = first[t][0]
        ends_ref[1, t] = v_ref[t, pl.ds(rows - 1, 8, stride=rows), :]
        ends_ref[2, t] = first[t][1]
        ends_ref[3, t] = w_ref[t, pl.ds(rows - 1, 8, stride=rows), :]


def span_modes(x_ref, table, mode):
    planes = x_ref.shape[0] // 8
    both = [
        jnp.transpose(x_ref[pl.ds(mode + p, planes, stride=8), :]) for p in range(2)
    ]
    x = jnp.concatenate(both, axis=0)
    return jnp.dot(parts(x, 1), table, preferred_element_type=f32)


def span_first_kernel(x_ref, t_ref, o_ref):
    tiles = o_ref.shape[0]
    for mode in range(0, 8, 2):
        y = span_modes(x_ref, t_ref[...], mode)
        for t in range(tiles):
            o_ref[t, mode * 128 : (mode + 2) * 128, :] = y[:, t * 128 : (t + 1) * 128]


def pair_copies(hbm, held, sems, first):
    out = []
    for pair in range(4):
        part = pl.ds(pair * 256, 256)
        out.append(
            pltpu.make_async_copy(hbm.at[:, part, :], held.at[:, part, :], sems.at[first + pair])
        )
    return out


def source_kernel(
    x_ref, weight_ref, gap_ref, t_hbm, s_hbm, v_hbm, w_hbm, o_ref, ends_ref, t, s, v, w, sems
):
    tiles = o_ref.shape[0]
    table = pltpu.make_async_copy(t_hbm, t, sems.at[0])
    table.start()
    copies = list(
        zip(
            pair_copies(s_hbm, s, sems, 1),
            pair_copies(v_hbm, v, sems, 5),
            pair_copies(w_hbm, w, sems, 9),
        )
    )
    for group in copies:
        for copy in group:
            copy.start()
    table.wait()
    weight = weight_ref[...]
    for pair in range(4):
        y = span_modes(x_ref, t[...], 2 * pair)
        for copy in copies[pair]:
            copy.wait()
        for p in range(2):
            mode = 2 * pair + p
            part = slice(mode * 128, (mode + 1) * 128)
            for tile in range(tiles):
                side = y[p * 128 : (p + 1) * 128, tile * 128 : (tile + 1) * 128] + s[tile, part, :]
                o_ref[tile, part, :] = side
                side = side * weight
                row = slice(mode, mode + 1)
                ends_ref[0, tile, row, :] = -gap_ref[0] * jnp.sum(
                    side * v[tile, part, :], axis=0, keepdims=True
                )
                ends_ref[1, tile, row, :] = -gap_ref[1] * jnp.sum(
                    side * w[tile, part, :], axis=0, keepdims=True
                )


def sweep_kernel(x_ref, inv_hbm, m_hbm, r_hbm, o_ref, inv, m, r, held, sems):
    tiles = o_ref.shape[0]
    rows = inv.shape[0]
    count = 4
    chunk = rows // count

    def copies(hbm, here, first):
        return [
            pltpu.make_async_copy(
                hbm.at[pl.ds(c * chunk, chunk)], here.at[pl.ds(c * chunk, chunk)], sems.at[first + c]
            )
            for c in range(count)
        ]

    invs, ms, rs = copies(inv_hbm, inv, 0), copies(m_hbm, m, count), copies(r_hbm, r, 2 * count)
    for c in range(count):
        invs[c].start()
        ms[c].start()
    for c in range(count - 1, -1, -1):
        rs[c].start()

    def ahead(block, carry):
        for j in range(8):
            y = block * 8 + j
            out = []
            for t in range(tiles):
                side = x_ref[t, pl.ds(y, 8, stride=rows), :]
                val = side * inv[y, t] - m[y, t] * carry[t]
                held[y, t] = val
                out.append(val)
            carry = tuple(out)
        return carry

    carry = (jnp.zeros((8, 128), f32),) * tiles
    for c in range(count):
        invs[c].wait()
        ms[c].wait()
        carry = lax.fori_loop(c * chunk // 8, (c + 1) * chunk // 8, ahead, carry)

    def back(step, carry):
        for j in range(8):
            y = rows - 1 - (step * 8 + j)
            out = []
            for t in range(tiles):
                val = held[y, t] - r[y, t] * carry[t]
                o_ref[t, pl.ds(y, 8, stride=rows), :] = val
                out.append(val)
            carry = tuple(out)
        return carry

    carry = (jnp.zeros((8, 128), f32),) * tiles
    for c in range(count):
        rs[count - 1 - c].wait()
        carry = lax.fori_loop(c * chunk // 8, (c + 1) * chunk // 8, back, carry)


def join_kernel(me_ref, y_ref, *refs):
    ends, (vw_ref, v_hbm, w_hbm, t_hbm, o_ref, ys_ref, b_ref, f_ref, v, w, t, sems) = (
        refs[:-12],
        refs[-12:],
    )
    blocks = vw_ref.shape[0]
    tiles = y_ref.shape[0]
    me = me_ref[0]
    table = pltpu.make_async_copy(t_hbm, t, sems.at[0])
    copies = list(zip(pair_copies(v_hbm, v, sems, 1), pair_copies(w_hbm, w, sems, 5)))
    for copy in copies[0]:
        copy.start()
    table.start()
    for group in copies[1:]:
        for copy in group:
            copy.start()
    for shift in range(blocks):
        ys_ref[shift] = ends[shift][...]
    for tile in range(tiles):
        alpha = jnp.zeros((8, 128), f32)
        beta = jnp.zeros((8, 128), f32)
        alphas, betas, starts, scales = [], [], [], []
        for g in range(blocks):
            slot = lax.rem(me + blocks - g, blocks)
            yf = ys_ref[slot, 0, tile]
            yb = ys_ref[slot, 1, tile]
            vf, vb, wf, wb = (vw_ref[slot, n, tile] for n in range(4))
            scale = 1.0 / (1.0 - vf * beta)
            start = (yf + vf * alpha) * scale
            starts.append(start)
            scales.append(wf * scale)
            alpha, beta = (
                yb + vb * (alpha + beta * start),
                wb + vb * beta * wf * scale,
            )
            alphas.append(alpha)
            betas.append(beta)
        after = jnp.zeros((8, 128), f32)
        f_ref[blocks, tile] = after
        b_ref[0, tile] = after
        for g in range(blocks - 1, -1, -1):
            b_ref[g + 1, tile] = alphas[g] + betas[g] * after
            after = starts[g] + scales[g] * after
            f_ref[g, tile] = after
    for pair in range(4):
        for copy in copies[pair]:
            copy.wait()
        if pair == 0:
            table.wait()
        columns = []
        for tile in range(tiles):
            both = []
            for p in range(2):
                mode = 2 * pair + p
                part = slice(mode * 128, (mode + 1) * 128)
                left = b_ref[me, tile, pl.ds(mode, 1), :]
                right = f_ref[me + 1, tile, pl.ds(mode, 1), :]
                both.append(
                    y_ref[tile, part, :] + v[tile, part, :] * left + w[tile, part, :] * right
                )
            columns.append(jnp.concatenate(both, axis=0))
        x = jnp.concatenate(columns, axis=1)
        y = lax.dot_general(
            t[...], parts(x, 1), (((1,), (1,)), ((), ())), preferred_element_type=f32
        )
        for p in range(2):
            part = y[:, 128 * p : 128 * (p + 1)]
            o_ref[:, 2 * pair + p] = part.reshape(part.shape[0] // 8, 8, 128)


def flow_inverse_kernel(x_ref, t_ref, o_ref):
    slots = x_ref.shape[0] // 8
    plane = pl.program_id(0) * 2
    x = jnp.concatenate([x_ref[pl.ds(plane + p, slots, stride=8), :] for p in range(2)], axis=1)
    y = jnp.dot(t_ref[...], parts(x, 0), preferred_element_type=f32)
    for p in range(2):
        o_ref[p] = y[:, 128 * p : 128 * (p + 1)]


def local(velocity, spacing):
    planes, flow_length, rows = velocity.shape[1:]
    size_x = lax.axis_size("gx")
    size_z = lax.axis_size("gz")
    blocks = lax.axis_size("gy")
    group = size_x * size_z
    span_length = planes * group
    modes = flow_length // group
    tiles = span_length // 128
    flow_forward, flow_derive, flow_inverse, flow_square = np_tables(flow_length, 1.0)
    span_forward, span_derive, span_inverse, span_square = np_tables(span_length, span_step)
    field_flops = 2 * 3 * planes * rows * flow_length * flow_length
    field_bytes = 4 * planes * rows * flow_length
    me = lax.axis_index("gy")
    both = ("gx", "gz")

    def moved(x):
        return lax.all_to_all(x, both, split_axis=0, concat_axis=0, tiled=True)

    field_shape = jax.ShapeDtypeStruct((group, planes, modes, rows), f32)
    table = jnp.asarray(left_table(flow_forward.T))
    plane_block = lambda c: pl.BlockSpec((1, 2, flow_length, rows), lambda i: (c, i, 0, 0))
    whole = lambda *shape: pl.BlockSpec(shape, lambda i: (0,) * len(shape))
    out_block = pl.BlockSpec((group, 2, modes, rows), lambda i: (0, i, 0, 0))
    span_sent = pl.pallas_call(
        span_field_kernel,
        grid=(planes // 2,),
        in_specs=[plane_block(2), whole(*table.shape)],
        out_specs=out_block,
        out_shape=field_shape,
        compiler_params=params(58),
        cost_estimate=cost(field_flops, 2 * field_bytes),
        name="span_field",
    )(velocity, table)
    span_here = moved(span_sent)

    v = velocity[1]
    up = [(i, i + 1) for i in range(blocks - 1)]
    down = [(j, i) for i, j in up]
    before = lax.ppermute(v[:, :, rows - 1], "gy", up)
    after = lax.ppermute(v[:, :, 0], "gy", down)
    gaps = lax.dynamic_slice_in_dim(spacing, me * rows, rows + 1)
    width = gaps[:-1] + gaps[1:]
    lower = 2.0 / (width * gaps[:-1])
    upper = 2.0 / (width * gaps[1:])
    flow_table = jnp.asarray(
        np.concatenate([left_table(flow_derive.T), left_table(flow_forward.T)], axis=1)
    )
    flow_sent = pl.pallas_call(
        flow_field_kernel,
        grid=(planes // 2,),
        in_specs=[
            plane_block(0),
            plane_block(1),
            whole(planes, flow_length),
            whole(planes, flow_length),
            whole(1, rows),
            whole(*flow_table.shape),
        ],
        out_specs=out_block,
        out_shape=field_shape,
        compiler_params=params(58),
        cost_estimate=cost(2 * field_flops, 3 * field_bytes),
        name="flow_field",
    )(velocity, velocity, before, after, width.reshape(1, rows), flow_table)
    flow_here = moved(flow_sent)

    first_mode = (lax.axis_index("gx") * size_z + lax.axis_index("gz")) * modes
    mode_square = lax.dynamic_slice_in_dim(jnp.asarray(flow_square), first_mode, modes)
    sigma = mode_square[None, :, None] + jnp.asarray(span_square).reshape(tiles, 1, 128)
    step_shape = jax.ShapeDtypeStruct((rows, tiles, modes, 128), f32)
    slab_shape = jax.ShapeDtypeStruct((tiles, modes * rows, 128), f32)
    vmem = pl.BlockSpec(memory_space=pltpu.VMEM)
    smem = pl.BlockSpec(memory_space=pltpu.SMEM)
    inv, m, r, v_all, w_all, vw_ends = pl.pallas_call(
        factor_kernel,
        in_specs=[smem, smem, vmem],
        out_specs=[vmem] * 6,
        out_shape=[step_shape] * 3
        + [slab_shape] * 2
        + [jax.ShapeDtypeStruct((4, tiles, modes, 128), f32)],
        compiler_params=params(58),
        cost_estimate=cost(field_flops, 5 * field_bytes),
        name="factor",
    )(lower, upper, sigma)
    rings = [[(i, (i + n) % blocks) for i in range(blocks)] for n in range(1, blocks)]
    vw = jnp.stack([vw_ends] + [lax.ppermute(vw_ends, "gy", ring) for ring in rings])
    span_here, vw = lax.optimization_barrier((span_here, vw))

    flat = (span_length * modes, rows)
    hbm = pl.BlockSpec(memory_space=pltpu.HBM)
    span_source = pl.pallas_call(
        span_first_kernel,
        in_specs=[vmem, vmem],
        out_specs=vmem,
        out_shape=slab_shape,
        compiler_params=params(58),
        cost_estimate=cost(field_flops, 2 * field_bytes),
        name="span_first",
    )(span_here.reshape(flat), jnp.asarray(right_table(span_derive)))
    slab = pltpu.VMEM(slab_shape.shape, f32)
    weight = jnp.broadcast_to((0.5 * width)[:, None], (rows, 128))
    end_gaps = jnp.stack([gaps[0], gaps[rows]])
    source, y_ends = pl.pallas_call(
        source_kernel,
        in_specs=[vmem, vmem, smem] + [hbm] * 4,
        out_specs=[vmem] * 2,
        out_shape=[slab_shape, jax.ShapeDtypeStruct((2, tiles, modes, 128), f32)],
        scratch_shapes=[
            pltpu.VMEM((3 * span_length, span_length), bf16),
            slab,
            slab,
            slab,
            pltpu.SemaphoreType.DMA((13,)),
        ],
        compiler_params=params(32),
        cost_estimate=cost(field_flops, 5 * field_bytes),
        name="source",
    )(
        flow_here.reshape(flat),
        weight,
        end_gaps,
        jnp.asarray(right_table(span_forward)),
        span_source,
        v_all,
        w_all,
    )
    ends = [y_ends] + [lax.ppermute(y_ends, "gy", ring) for ring in rings]
    step = pltpu.VMEM(step_shape.shape, f32)
    y_all = pl.pallas_call(
        sweep_kernel,
        in_specs=[vmem] + [hbm] * 3,
        out_specs=vmem,
        out_shape=slab_shape,
        scratch_shapes=[step] * 4 + [pltpu.SemaphoreType.DMA((12,))],
        compiler_params=params(32),
        cost_estimate=cost(field_flops, 5 * field_bytes),
        name="sweep",
    )(source, inv, m, r)
    end_shape = (blocks + 1, tiles, modes, 128)
    back_sent = pl.pallas_call(
        join_kernel,
        in_specs=[smem] + [vmem] * (2 + blocks) + [hbm] * 3,
        out_specs=vmem,
        out_shape=jax.ShapeDtypeStruct((group, modes, planes, rows), f32),
        scratch_shapes=[
            pltpu.VMEM((blocks, 2, tiles, modes, 128), f32),
            pltpu.VMEM(end_shape, f32),
            pltpu.VMEM(end_shape, f32),
            slab,
            slab,
            pltpu.VMEM((span_length, 3 * span_length), bf16),
            pltpu.SemaphoreType.DMA((9,)),
        ],
        compiler_params=params(32),
        cost_estimate=cost(field_flops, 4 * field_bytes),
        name="join",
    )(
        me.reshape(1).astype(jnp.int32),
        y_all,
        *ends,
        vw,
        v_all,
        w_all,
        jnp.asarray(left_table(span_inverse.T)),
    )
    back_here = moved(back_sent)
    last_table = jnp.asarray(left_table(flow_inverse.T))
    return pl.pallas_call(
        flow_inverse_kernel,
        grid=(planes // 2,),
        in_specs=[whole(flow_length * planes, rows), whole(*last_table.shape)],
        out_specs=pl.BlockSpec((2, flow_length, rows), lambda i: (i, 0, 0)),
        out_shape=jax.ShapeDtypeStruct((planes, flow_length, rows), f32),
        compiler_params=params(32),
        cost_estimate=cost(field_flops, 2 * field_bytes),
        name="flow_inverse",
    )(back_here.reshape(flow_length * planes, rows), last_table)


def solution(mesh):
    return jax.shard_map(
        local,
        mesh=mesh,
        in_specs=(P(None, ("gx", "gz"), None, "gy"), P()),
        out_specs=P(("gx", "gz"), None, "gy"),
        check_vma=False,
    )
```

```python
import functools
import math

import jax
import jax.numpy as jnp
import ml_dtypes
import numpy as np
from jax import lax
from jax.experimental import pallas as pl
from jax.experimental.pallas import tpu as pltpu
from jax.sharding import PartitionSpec as P

span_step = 0.5
f32 = jnp.float32
bf16 = jnp.bfloat16


def np_tables(length, step_size):
    index = np.arange(length)
    wave = np.where(index == 1, length // 2, index // 2)
    phase = (index[:, None] * wave[None, :]) % length
    angle = 2.0 * math.pi / length * phase
    odd_high = np.logical_and(index % 2 == 1, index >= 3)[None, :]
    forward = np.where(odd_high, -np.sin(angle), np.cos(angle))
    kappa = 2.0 * math.pi / (length * step_size) * wave
    scale = np.where(index >= 2, kappa, 0.0)[None, :]
    derive = np.where(odd_high, np.cos(angle), np.sin(angle)) * scale
    weight = np.where(index >= 2, 2.0, 1.0) / length
    inverse = forward * weight[None, :]
    order = np.argsort(wave % 2, kind="stable")
    square = (kappa * kappa).astype(np.float32)
    return forward[:, order], derive[:, order], inverse[:, order], square[order]


def halved(table):
    half = table.shape[0] // 2
    return table[:half, :half], table[:half, half:]


def split_np(table):
    high = table.astype(np.float32).astype(ml_dtypes.bfloat16)
    low = (table - high.astype(np.float64)).astype(np.float32).astype(ml_dtypes.bfloat16)
    return high, low


def thrice(table, axis):
    high, low = split_np(table)
    return np.concatenate([high, low, high], axis=axis)


def slots_left(table):
    return np.stack([thrice(part.T, 1) for part in halved(table)])


def slots_right(table):
    return np.stack([thrice(part, 0) for part in halved(table)])


def nodes_left(table):
    return np.stack([thrice(part, 1) for part in halved(table)])


def parts(x, axis):
    high = x.astype(bf16)
    low = (x - high.astype(f32)).astype(bf16)
    return jnp.concatenate([high, high, low], axis=axis)


def folded(x, axis):
    half = x.shape[axis] // 2
    first = lax.slice_in_dim(x, 0, half, axis=axis)
    second = lax.slice_in_dim(x, half, 2 * half, axis=axis)
    return parts(first + second, axis), parts(first - second, axis)


def to_nodes(even, odd):
    return jnp.concatenate([even + odd, even - odd], axis=0)


def dot(a, b):
    return jnp.dot(a, b, preferred_element_type=f32)


def params(mib):
    return pltpu.CompilerParams(vmem_limit_bytes=mib * 1024 * 1024)


def cost(flops, size):
    return pl.CostEstimate(flops=flops, bytes_accessed=size, transcendentals=0)


def span_field_kernel(w_ref, t_ref, o_ref):
    x = jnp.concatenate([w_ref[0, 0], w_ref[0, 1]], axis=1)
    for k, part in enumerate(folded(x, 0)):
        store_modes(o_ref, k, dot(t_ref[k], part))


def store_modes(o_ref, k, y):
    owners = y.shape[0] // 8
    for p in range(2):
        part = y[:, 128 * p : 128 * (p + 1)].reshape(owners, 8, 128)
        o_ref[k * owners : (k + 1) * owners, p] = part


def flow_field_kernel(u_ref, v_ref, before_ref, after_ref, width_ref, t_ref, o_ref):
    step = pl.program_id(0)
    lane = lax.broadcasted_iota(jnp.int32, v_ref.shape[2:], 1)
    width = width_ref[...]
    slopes = []
    for p in range(2):
        v = v_ref[0, p]
        z = step * 2 + p
        before = jnp.transpose(jnp.broadcast_to(before_ref[pl.ds(z, 1), :], (128, v.shape[0])))
        after = jnp.transpose(jnp.broadcast_to(after_ref[pl.ds(z, 1), :], (128, v.shape[0])))
        down = jnp.where(lane == 0, before, pltpu.roll(v, 1, 1))
        up = jnp.where(lane == 127, after, pltpu.roll(v, 127, 1))
        slopes.append((up - down) / width)
    u = jnp.concatenate([u_ref[0, 0], u_ref[0, 1]], axis=1)
    s = jnp.concatenate(slopes, axis=1)
    for k, pair in enumerate(zip(folded(u, 0), folded(s, 0))):
        store_modes(o_ref, k, dot(t_ref[k], jnp.concatenate(pair, axis=0)))


def factor_kernel(low_ref, up_ref, sigma_ref, inv_ref, v_ref, w_ref, ends_ref):
    rows = inv_ref.shape[0]
    tiles = inv_ref.shape[1]

    def ahead(y, carry):
        low = low_ref[y]
        up = up_ref[y]
        out = []
        for t in range(tiles):
            r, val = carry[t]
            inv = 1.0 / (-(low + up) - sigma_ref[t] - low * r)
            val = -(low * inv) * val
            inv_ref[y, t] = inv
            v_ref[t, pl.ds(y, 8, stride=rows), :] = val
            out.append((up * inv, val))
        return tuple(out)

    zero = jnp.zeros((8, 128), f32)
    one = jnp.ones((8, 128), f32)
    lax.fori_loop(0, rows, ahead, ((zero, one),) * tiles)

    def back(s, carry):
        y = rows - 1 - s
        out = []
        for t in range(tiles):
            v, w = carry[t]
            r = up_ref[y] * inv_ref[y, t]
            v = v_ref[t, pl.ds(y, 8, stride=rows), :] - r * v
            w = -r * w
            v_ref[t, pl.ds(y, 8, stride=rows), :] = v
            w_ref[t, pl.ds(y, 8, stride=rows), :] = w
            out.append((v, w))
        return tuple(out)

    first = lax.fori_loop(0, rows, back, ((zero, one),) * tiles)
    for t in range(tiles):
        ends_ref[0, t] = first[t][0]
        ends_ref[1, t] = v_ref[t, pl.ds(rows - 1, 8, stride=rows), :]
        ends_ref[2, t] = first[t][1]
        ends_ref[3, t] = w_ref[t, pl.ds(rows - 1, 8, stride=rows), :]


def span_modes(x_ref, t_ref, mode):
    planes = x_ref.shape[0] // 8
    both = [
        jnp.transpose(x_ref[pl.ds(mode + p, planes, stride=8), :]) for p in range(2)
    ]
    x = jnp.concatenate(both, axis=0)
    return jnp.concatenate([dot(part, t_ref[k]) for k, part in enumerate(folded(x, 1))], axis=1)


def span_first_kernel(x_ref, t_ref, o_ref):
    tiles = o_ref.shape[0]
    for mode in range(0, 8, 2):
        y = span_modes(x_ref, t_ref, mode)
        for t in range(tiles):
            o_ref[t, mode * 128 : (mode + 2) * 128, :] = y[:, t * 128 : (t + 1) * 128]


def pair_copies(hbm, held, sems, first):
    out = []
    for pair in range(4):
        part = pl.ds(pair * 256, 256)
        out.append(
            pltpu.make_async_copy(hbm.at[:, part, :], held.at[:, part, :], sems.at[first + pair])
        )
    return out


def source_kernel(
    x_ref, weight_ref, gap_ref, t_hbm, s_hbm, v_hbm, w_hbm, o_ref, ends_ref, t, s, v, w, sems
):
    tiles = o_ref.shape[0]
    table = pltpu.make_async_copy(t_hbm, t, sems.at[0])
    table.start()
    copies = list(
        zip(
            pair_copies(s_hbm, s, sems, 1),
            pair_copies(v_hbm, v, sems, 5),
            pair_copies(w_hbm, w, sems, 9),
        )
    )
    for group in copies:
        for copy in group:
            copy.start()
    table.wait()
    weight = weight_ref[...]
    for pair in range(4):
        y = span_modes(x_ref, t, 2 * pair)
        for copy in copies[pair]:
            copy.wait()
        for p in range(2):
            mode = 2 * pair + p
            part = slice(mode * 128, (mode + 1) * 128)
            for tile in range(tiles):
                side = y[p * 128 : (p + 1) * 128, tile * 128 : (tile + 1) * 128] + s[tile, part, :]
                o_ref[tile, part, :] = side
                side = side * weight
                row = slice(mode, mode + 1)
                ends_ref[0, tile, row, :] = -gap_ref[0] * jnp.sum(
                    side * v[tile, part, :], axis=0, keepdims=True
                )
                ends_ref[1, tile, row, :] = -gap_ref[1] * jnp.sum(
                    side * w[tile, part, :], axis=0, keepdims=True
                )


def sweep_kernel(low_ref, up_ref, x_ref, inv_hbm, o_ref, inv, held, sems):
    tiles = o_ref.shape[0]
    rows = inv.shape[0]
    count = 4
    chunk = rows // count
    copies = [
        pltpu.make_async_copy(
            inv_hbm.at[pl.ds(c * chunk, chunk)], inv.at[pl.ds(c * chunk, chunk)], sems.at[c]
        )
        for c in range(count)
    ]
    for copy in copies:
        copy.start()

    def ahead(block, carry):
        for j in range(8):
            y = block * 8 + j
            low = low_ref[y]
            out = []
            for t in range(tiles):
                scale = inv[y, t]
                side = x_ref[t, pl.ds(y, 8, stride=rows), :]
                val = side * scale - (low * scale) * carry[t]
                held[y, t] = val
                out.append(val)
            carry = tuple(out)
        return carry

    carry = (jnp.zeros((8, 128), f32),) * tiles
    for c in range(count):
        copies[c].wait()
        carry = lax.fori_loop(c * chunk // 8, (c + 1) * chunk // 8, ahead, carry)

    def back(step, carry):
        for j in range(8):
            y = rows - 1 - (step * 8 + j)
            up = up_ref[y]
            out = []
            for t in range(tiles):
                val = held[y, t] - (up * inv[y, t]) * carry[t]
                o_ref[t, pl.ds(y, 8, stride=rows), :] = val
                out.append(val)
            carry = tuple(out)
        return carry

    lax.fori_loop(0, rows // 8, back, (jnp.zeros((8, 128), f32),) * tiles)


def join_kernel(me_ref, y_ref, *refs):
    ends, (vw_ref, v_hbm, w_hbm, t_hbm, o_ref, ys_ref, b_ref, f_ref, v, w, t, sems) = (
        refs[:-12],
        refs[-12:],
    )
    blocks = vw_ref.shape[0]
    tiles = y_ref.shape[0]
    me = me_ref[0]
    table = pltpu.make_async_copy(t_hbm, t, sems.at[0])
    copies = list(zip(pair_copies(v_hbm, v, sems, 1), pair_copies(w_hbm, w, sems, 5)))
    for copy in copies[0]:
        copy.start()
    table.start()
    for group in copies[1:]:
        for copy in group:
            copy.start()
    for shift in range(blocks):
        ys_ref[shift] = ends[shift][...]
    for tile in range(tiles):
        alpha = jnp.zeros((8, 128), f32)
        beta = jnp.zeros((8, 128), f32)
        alphas, betas, starts, scales = [], [], [], []
        for g in range(blocks):
            slot = lax.rem(me + blocks - g, blocks)
            yf = ys_ref[slot, 0, tile]
            yb = ys_ref[slot, 1, tile]
            vf, vb, wf, wb = (vw_ref[slot, n, tile] for n in range(4))
            scale = 1.0 / (1.0 - vf * beta)
            start = (yf + vf * alpha) * scale
            starts.append(start)
            scales.append(wf * scale)
            alpha, beta = (
                yb + vb * (alpha + beta * start),
                wb + vb * beta * wf * scale,
            )
            alphas.append(alpha)
            betas.append(beta)
        after = jnp.zeros((8, 128), f32)
        f_ref[blocks, tile] = after
        b_ref[0, tile] = after
        for g in range(blocks - 1, -1, -1):
            b_ref[g + 1, tile] = alphas[g] + betas[g] * after
            after = starts[g] + scales[g] * after
            f_ref[g, tile] = after
    for pair in range(4):
        for copy in copies[pair]:
            copy.wait()
        if pair == 0:
            table.wait()
        columns = []
        for tile in range(tiles):
            both = []
            for p in range(2):
                mode = 2 * pair + p
                part = slice(mode * 128, (mode + 1) * 128)
                left = b_ref[me, tile, pl.ds(mode, 1), :]
                right = f_ref[me + 1, tile, pl.ds(mode, 1), :]
                both.append(
                    y_ref[tile, part, :] + v[tile, part, :] * left + w[tile, part, :] * right
                )
            columns.append(jnp.concatenate(both, axis=0))
        half = tiles // 2
        y = to_nodes(
            *(
                lax.dot_general(
                    t[k],
                    parts(jnp.concatenate(columns[k * half : (k + 1) * half], axis=1), 1),
                    (((1,), (1,)), ((), ())),
                    preferred_element_type=f32,
                )
                for k in range(2)
            )
        )
        for p in range(2):
            part = y[:, 128 * p : 128 * (p + 1)]
            o_ref[:, 2 * pair + p] = part.reshape(part.shape[0] // 8, 8, 128)


def flow_inverse_kernel(x_ref, t_ref, o_ref):
    slots = x_ref.shape[0] // 8
    plane = pl.program_id(0) * 2
    x = jnp.concatenate([x_ref[pl.ds(plane + p, slots, stride=8), :] for p in range(2)], axis=1)
    half = slots // 2
    y = to_nodes(*(dot(t_ref[k], parts(x[k * half : (k + 1) * half], 0)) for k in range(2)))
    for p in range(2):
        o_ref[p] = y[:, 128 * p : 128 * (p + 1)]


def local(velocity, spacing):
    planes, flow_length, rows = velocity.shape[1:]
    size_x = lax.axis_size("gx")
    size_z = lax.axis_size("gz")
    blocks = lax.axis_size("gy")
    group = size_x * size_z
    span_length = planes * group
    modes = flow_length // group
    tiles = span_length // 128
    flow_forward, flow_derive, flow_inverse, flow_square = np_tables(flow_length, 1.0)
    span_forward, span_derive, span_inverse, span_square = np_tables(span_length, span_step)
    field_flops = 2 * 3 * planes * rows * flow_length * flow_length
    field_bytes = 4 * planes * rows * flow_length
    me = lax.axis_index("gy")
    both = ("gx", "gz")

    def moved(x):
        return lax.all_to_all(x, both, split_axis=0, concat_axis=0, tiled=True)

    field_shape = jax.ShapeDtypeStruct((group, planes, modes, rows), f32)
    table = jnp.asarray(slots_left(flow_forward))
    plane_block = lambda c: pl.BlockSpec((1, 2, flow_length, rows), lambda i: (c, i, 0, 0))
    whole = lambda *shape: pl.BlockSpec(shape, lambda i: (0,) * len(shape))
    out_block = pl.BlockSpec((group, 2, modes, rows), lambda i: (0, i, 0, 0))
    span_sent = pl.pallas_call(
        span_field_kernel,
        grid=(planes // 2,),
        in_specs=[plane_block(2), whole(*table.shape)],
        out_specs=out_block,
        out_shape=field_shape,
        compiler_params=params(58),
        cost_estimate=cost(field_flops, 2 * field_bytes),
        name="span_field",
    )(velocity, table)
    span_here = moved(span_sent)

    v = velocity[1]
    up = [(i, i + 1) for i in range(blocks - 1)]
    down = [(j, i) for i, j in up]
    before = lax.ppermute(v[:, :, rows - 1], "gy", up)
    after = lax.ppermute(v[:, :, 0], "gy", down)
    gaps = lax.dynamic_slice_in_dim(spacing, me * rows, rows + 1)
    width = gaps[:-1] + gaps[1:]
    lower = 2.0 / (width * gaps[:-1])
    upper = 2.0 / (width * gaps[1:])
    flow_table = jnp.asarray(
        np.concatenate([slots_left(flow_derive), slots_left(flow_forward)], axis=2)
    )
    flow_sent = pl.pallas_call(
        flow_field_kernel,
        grid=(planes // 2,),
        in_specs=[
            plane_block(0),
            plane_block(1),
            whole(planes, flow_length),
            whole(planes, flow_length),
            whole(1, rows),
            whole(*flow_table.shape),
        ],
        out_specs=out_block,
        out_shape=field_shape,
        compiler_params=params(58),
        cost_estimate=cost(2 * field_flops, 3 * field_bytes),
        name="flow_field",
    )(velocity, velocity, before, after, width.reshape(1, rows), flow_table)
    flow_here = moved(flow_sent)

    first_mode = (lax.axis_index("gx") * size_z + lax.axis_index("gz")) * modes
    mode_square = lax.dynamic_slice_in_dim(jnp.asarray(flow_square), first_mode, modes)
    sigma = mode_square[None, :, None] + jnp.asarray(span_square).reshape(tiles, 1, 128)
    step_shape = jax.ShapeDtypeStruct((rows, tiles, modes, 128), f32)
    slab_shape = jax.ShapeDtypeStruct((tiles, modes * rows, 128), f32)
    vmem = pl.BlockSpec(memory_space=pltpu.VMEM)
    smem = pl.BlockSpec(memory_space=pltpu.SMEM)
    inv, v_all, w_all, vw_ends = pl.pallas_call(
        factor_kernel,
        in_specs=[smem, smem, vmem],
        out_specs=[vmem] * 4,
        out_shape=[step_shape]
        + [slab_shape] * 2
        + [jax.ShapeDtypeStruct((4, tiles, modes, 128), f32)],
        compiler_params=params(58),
        cost_estimate=cost(field_flops, 3 * field_bytes),
        name="factor",
    )(lower, upper, sigma)
    rings = [[(i, (i + n) % blocks) for i in range(blocks)] for n in range(1, blocks)]
    vw = jnp.stack([vw_ends] + [lax.ppermute(vw_ends, "gy", ring) for ring in rings])
    weight = jnp.broadcast_to((0.5 * width)[:, None], (rows, 128))
    end_gaps = jnp.stack([gaps[0], gaps[rows]])
    span_here, vw, weight, end_gaps = lax.optimization_barrier((span_here, vw, weight, end_gaps))

    flat = (span_length * modes, rows)
    hbm = pl.BlockSpec(memory_space=pltpu.HBM)
    span_source = pl.pallas_call(
        span_first_kernel,
        in_specs=[vmem, vmem],
        out_specs=vmem,
        out_shape=slab_shape,
        compiler_params=params(58),
        cost_estimate=cost(field_flops, 2 * field_bytes),
        name="span_first",
    )(span_here.reshape(flat), jnp.asarray(slots_right(span_derive)))
    slab = pltpu.VMEM(slab_shape.shape, f32)
    source, y_ends = pl.pallas_call(
        source_kernel,
        in_specs=[vmem, vmem, smem] + [hbm] * 4,
        out_specs=[vmem] * 2,
        out_shape=[slab_shape, jax.ShapeDtypeStruct((2, tiles, modes, 128), f32)],
        scratch_shapes=[
            pltpu.VMEM((2, 3 * span_length // 2, span_length // 2), bf16),
            slab,
            slab,
            slab,
            pltpu.SemaphoreType.DMA((13,)),
        ],
        compiler_params=params(48),
        cost_estimate=cost(field_flops, 5 * field_bytes),
        name="source",
    )(
        flow_here.reshape(flat),
        weight,
        end_gaps,
        jnp.asarray(slots_right(span_forward)),
        span_source,
        v_all,
        w_all,
    )
    ends = [y_ends] + [lax.ppermute(y_ends, "gy", ring) for ring in rings]
    step = pltpu.VMEM(step_shape.shape, f32)
    y_all = pl.pallas_call(
        sweep_kernel,
        in_specs=[smem, smem, vmem, hbm],
        out_specs=vmem,
        out_shape=slab_shape,
        scratch_shapes=[step] * 2 + [pltpu.SemaphoreType.DMA((4,))],
        compiler_params=params(32),
        cost_estimate=cost(field_flops, 3 * field_bytes),
        name="sweep",
    )(lower, upper, source, inv)
    end_shape = (blocks + 1, tiles, modes, 128)
    back_sent = pl.pallas_call(
        join_kernel,
        in_specs=[smem] + [vmem] * (2 + blocks) + [hbm] * 3,
        out_specs=vmem,
        out_shape=jax.ShapeDtypeStruct((group, modes, planes, rows), f32),
        scratch_shapes=[
            pltpu.VMEM((blocks, 2, tiles, modes, 128), f32),
            pltpu.VMEM(end_shape, f32),
            pltpu.VMEM(end_shape, f32),
            slab,
            slab,
            pltpu.VMEM((2, span_length // 2, 3 * span_length // 2), bf16),
            pltpu.SemaphoreType.DMA((9,)),
        ],
        compiler_params=params(32),
        cost_estimate=cost(field_flops, 4 * field_bytes),
        name="join",
    )(
        me.reshape(1).astype(jnp.int32),
        y_all,
        *ends,
        vw,
        v_all,
        w_all,
        jnp.asarray(nodes_left(span_inverse)),
    )
    back_here = moved(back_sent)
    last_table = jnp.asarray(nodes_left(flow_inverse))
    return pl.pallas_call(
        flow_inverse_kernel,
        grid=(planes // 2,),
        in_specs=[whole(flow_length * planes, rows), whole(*last_table.shape)],
        out_specs=pl.BlockSpec((2, flow_length, rows), lambda i: (i, 0, 0)),
        out_shape=jax.ShapeDtypeStruct((planes, flow_length, rows), f32),
        compiler_params=params(32),
        cost_estimate=cost(field_flops, 2 * field_bytes),
        name="flow_inverse",
    )(back_here.reshape(flow_length * planes, rows), last_table)


def solution(mesh):
    return jax.shard_map(
        local,
        mesh=mesh,
        in_specs=(P(None, ("gx", "gz"), None, "gy"), P()),
        out_specs=P(("gx", "gz"), None, "gy"),
        check_vma=False,
    )
```

```python
import functools
import math

import jax
import jax.numpy as jnp
import ml_dtypes
import numpy as np
from jax import lax
from jax.experimental import pallas as pl
from jax.experimental.pallas import tpu as pltpu
from jax.sharding import PartitionSpec as P

span_step = 0.5
f32 = jnp.float32
bf16 = jnp.bfloat16


def np_tables(length, step_size):
    index = np.arange(length)
    wave = np.where(index == 1, length // 2, index // 2)
    phase = (index[:, None] * wave[None, :]) % length
    angle = 2.0 * math.pi / length * phase
    odd_high = np.logical_and(index % 2 == 1, index >= 3)[None, :]
    forward = np.where(odd_high, -np.sin(angle), np.cos(angle))
    kappa = 2.0 * math.pi / (length * step_size) * wave
    scale = np.where(index >= 2, kappa, 0.0)[None, :]
    derive = np.where(odd_high, np.cos(angle), np.sin(angle)) * scale
    weight = np.where(index >= 2, 2.0, 1.0) / length
    inverse = forward * weight[None, :]
    order = np.argsort(wave % 2, kind="stable")
    square = (kappa * kappa).astype(np.float32)
    return forward[:, order], derive[:, order], inverse[:, order], square[order]


def halved(table):
    half = table.shape[0] // 2
    return table[:half, :half], table[:half, half:]


def split_np(table):
    high = table.astype(np.float32).astype(ml_dtypes.bfloat16)
    low = (table - high.astype(np.float64)).astype(np.float32).astype(ml_dtypes.bfloat16)
    return high, low


def thrice(table, axis):
    high, low = split_np(table)
    return np.concatenate([high, low, high], axis=axis)


def slots_left(table):
    return np.stack([thrice(part.T, 1) for part in halved(table)])


def slots_right(table):
    return np.stack([thrice(part, 0) for part in halved(table)])


def nodes_left(table):
    return np.stack([thrice(part, 1) for part in halved(table)])


def parts(x, axis):
    high = x.astype(bf16)
    low = (x - high.astype(f32)).astype(bf16)
    return jnp.concatenate([high, high, low], axis=axis)


def folded(x, axis):
    half = x.shape[axis] // 2
    first = lax.slice_in_dim(x, 0, half, axis=axis)
    second = lax.slice_in_dim(x, half, 2 * half, axis=axis)
    return parts(first + second, axis), parts(first - second, axis)


def to_nodes(even, odd):
    return jnp.concatenate([even + odd, even - odd], axis=0)


def dot(a, b):
    return jnp.dot(a, b, preferred_element_type=f32)


def params(mib):
    return pltpu.CompilerParams(vmem_limit_bytes=mib * 1024 * 1024)


def cost(flops, size):
    return pl.CostEstimate(flops=flops, bytes_accessed=size, transcendentals=0)


def span_field_kernel(w_hbm, t_hbm, o_hbm, w, t, o, sems):
    loads, stores = [], []
    for pair in range(4):
        part = pl.ds(2 * pair, 2)
        loads.append(pltpu.make_async_copy(w_hbm.at[2, part], w.at[part], sems.at[pair]))
        stores.append(pltpu.make_async_copy(o.at[:, part], o_hbm.at[:, part], sems.at[4 + pair]))
    tables = [pltpu.make_async_copy(t_hbm.at[k], t.at[k], sems.at[8 + k]) for k in range(2)]
    loads[0].start()
    for copy in tables + loads[1:]:
        copy.start()
    for pair in range(4):
        loads[pair].wait()
        x = jnp.concatenate([w[2 * pair], w[2 * pair + 1]], axis=1)
        for k, part in enumerate(folded(x, 0)):
            if pair == 0:
                tables[k].wait()
            store_modes(o.at[:, 2 * pair : 2 * pair + 2], k, dot(t[k], part))
        stores[pair].start()
    for copy in stores:
        copy.wait()


def store_modes(o_ref, k, y):
    owners = y.shape[0] // 8
    for p in range(2):
        part = y[:, 128 * p : 128 * (p + 1)].reshape(owners, 8, 128)
        o_ref[k * owners : (k + 1) * owners, p] = part


def flow_field_kernel(u_ref, v_ref, before_ref, after_ref, width_ref, t_ref, o_ref):
    step = pl.program_id(0)
    lane = lax.broadcasted_iota(jnp.int32, v_ref.shape[2:], 1)
    width = width_ref[...]
    slopes = []
    for p in range(2):
        v = v_ref[0, p]
        z = step * 2 + p
        before = jnp.transpose(jnp.broadcast_to(before_ref[pl.ds(z, 1), :], (128, v.shape[0])))
        after = jnp.transpose(jnp.broadcast_to(after_ref[pl.ds(z, 1), :], (128, v.shape[0])))
        down = jnp.where(lane == 0, before, pltpu.roll(v, 1, 1))
        up = jnp.where(lane == 127, after, pltpu.roll(v, 127, 1))
        slopes.append((up - down) / width)
    u = jnp.concatenate([u_ref[0, 0], u_ref[0, 1]], axis=1)
    s = jnp.concatenate(slopes, axis=1)
    for k, pair in enumerate(zip(folded(u, 0), folded(s, 0))):
        store_modes(o_ref, k, dot(t_ref[k], jnp.concatenate(pair, axis=0)))


def factor_kernel(low_ref, up_ref, sigma_ref, inv_ref, v_ref, w_ref, ends_ref):
    rows = inv_ref.shape[0]
    tiles = inv_ref.shape[1]

    def ahead(y, carry):
        low = low_ref[y]
        up = up_ref[y]
        out = []
        for t in range(tiles):
            r, val = carry[t]
            inv = 1.0 / (-(low + up) - sigma_ref[t] - low * r)
            val = -(low * inv) * val
            inv_ref[y, t] = inv
            v_ref[t, pl.ds(y, 8, stride=rows), :] = val
            out.append((up * inv, val))
        return tuple(out)

    zero = jnp.zeros((8, 128), f32)
    one = jnp.ones((8, 128), f32)
    lax.fori_loop(0, rows, ahead, ((zero, one),) * tiles)

    def back(s, carry):
        y = rows - 1 - s
        out = []
        for t in range(tiles):
            v, w = carry[t]
            r = up_ref[y] * inv_ref[y, t]
            v = v_ref[t, pl.ds(y, 8, stride=rows), :] - r * v
            w = -r * w
            v_ref[t, pl.ds(y, 8, stride=rows), :] = v
            w_ref[t, pl.ds(y, 8, stride=rows), :] = w
            out.append((v, w))
        return tuple(out)

    first = lax.fori_loop(0, rows, back, ((zero, one),) * tiles)
    for t in range(tiles):
        ends_ref[0, t] = first[t][0]
        ends_ref[1, t] = v_ref[t, pl.ds(rows - 1, 8, stride=rows), :]
        ends_ref[2, t] = first[t][1]
        ends_ref[3, t] = w_ref[t, pl.ds(rows - 1, 8, stride=rows), :]


def span_modes(x_ref, t_ref, mode):
    planes = x_ref.shape[0] // 8
    both = [
        jnp.transpose(x_ref[pl.ds(mode + p, planes, stride=8), :]) for p in range(2)
    ]
    x = jnp.concatenate(both, axis=0)
    return jnp.concatenate([dot(part, t_ref[k]) for k, part in enumerate(folded(x, 1))], axis=1)


def span_first_kernel(x_ref, t_ref, o_ref):
    tiles = o_ref.shape[0]
    for mode in range(0, 8, 2):
        y = span_modes(x_ref, t_ref, mode)
        for t in range(tiles):
            o_ref[t, mode * 128 : (mode + 2) * 128, :] = y[:, t * 128 : (t + 1) * 128]


def pair_copies(hbm, held, sems, first):
    out = []
    for pair in range(4):
        part = pl.ds(pair * 256, 256)
        out.append(
            pltpu.make_async_copy(hbm.at[:, part, :], held.at[:, part, :], sems.at[first + pair])
        )
    return out


def source_kernel(
    x_ref, weight_ref, gap_ref, t_hbm, s_hbm, v_hbm, w_hbm, o_ref, ends_ref, t, s, v, w, sems
):
    tiles = o_ref.shape[0]
    table = pltpu.make_async_copy(t_hbm, t, sems.at[0])
    table.start()
    copies = list(
        zip(
            pair_copies(s_hbm, s, sems, 1),
            pair_copies(v_hbm, v, sems, 5),
            pair_copies(w_hbm, w, sems, 9),
        )
    )
    for group in copies:
        for copy in group:
            copy.start()
    table.wait()
    weight = weight_ref[...]
    for pair in range(4):
        y = span_modes(x_ref, t, 2 * pair)
        for copy in copies[pair]:
            copy.wait()
        for p in range(2):
            mode = 2 * pair + p
            part = slice(mode * 128, (mode + 1) * 128)
            for tile in range(tiles):
                side = y[p * 128 : (p + 1) * 128, tile * 128 : (tile + 1) * 128] + s[tile, part, :]
                o_ref[tile, part, :] = side
                side = side * weight
                row = slice(mode, mode + 1)
                ends_ref[0, tile, row, :] = -gap_ref[0] * jnp.sum(
                    side * v[tile, part, :], axis=0, keepdims=True
                )
                ends_ref[1, tile, row, :] = -gap_ref[1] * jnp.sum(
                    side * w[tile, part, :], axis=0, keepdims=True
                )


def sweep_kernel(low_ref, up_ref, x_ref, inv_hbm, o_ref, inv, held, sems):
    tiles = o_ref.shape[0]
    rows = inv.shape[0]
    count = 4
    chunk = rows // count
    copies = [
        pltpu.make_async_copy(
            inv_hbm.at[pl.ds(c * chunk, chunk)], inv.at[pl.ds(c * chunk, chunk)], sems.at[c]
        )
        for c in range(count)
    ]
    for copy in copies:
        copy.start()

    def ahead(block, carry):
        for j in range(8):
            y = block * 8 + j
            low = low_ref[y]
            out = []
            for t in range(tiles):
                scale = inv[y, t]
                side = x_ref[t, pl.ds(y, 8, stride=rows), :]
                val = side * scale - (low * scale) * carry[t]
                held[y, t] = val
                out.append(val)
            carry = tuple(out)
        return carry

    carry = (jnp.zeros((8, 128), f32),) * tiles
    for c in range(count):
        copies[c].wait()
        carry = lax.fori_loop(c * chunk // 8, (c + 1) * chunk // 8, ahead, carry)

    def back(step, carry):
        for j in range(8):
            y = rows - 1 - (step * 8 + j)
            up = up_ref[y]
            out = []
            for t in range(tiles):
                val = held[y, t] - (up * inv[y, t]) * carry[t]
                o_ref[t, pl.ds(y, 8, stride=rows), :] = val
                out.append(val)
            carry = tuple(out)
        return carry

    lax.fori_loop(0, rows // 8, back, (jnp.zeros((8, 128), f32),) * tiles)


def join_kernel(me_ref, y_ref, *refs):
    ends, (vw_ref, v_hbm, w_hbm, t_hbm, o_ref, ys_ref, b_ref, f_ref, v, w, t, sems) = (
        refs[:-12],
        refs[-12:],
    )
    blocks = vw_ref.shape[0]
    tiles = y_ref.shape[0]
    me = me_ref[0]
    table = pltpu.make_async_copy(t_hbm, t, sems.at[0])
    copies = list(zip(pair_copies(v_hbm, v, sems, 1), pair_copies(w_hbm, w, sems, 5)))
    for copy in copies[0]:
        copy.start()
    table.start()
    for group in copies[1:]:
        for copy in group:
            copy.start()
    for shift in range(blocks):
        ys_ref[shift] = ends[shift][...]
    for tile in range(tiles):
        alpha = jnp.zeros((8, 128), f32)
        beta = jnp.zeros((8, 128), f32)
        alphas, betas, starts, scales = [], [], [], []
        for g in range(blocks):
            slot = lax.rem(me + blocks - g, blocks)
            yf = ys_ref[slot, 0, tile]
            yb = ys_ref[slot, 1, tile]
            vf, vb, wf, wb = (vw_ref[slot, n, tile] for n in range(4))
            scale = 1.0 / (1.0 - vf * beta)
            start = (yf + vf * alpha) * scale
            starts.append(start)
            scales.append(wf * scale)
            alpha, beta = (
                yb + vb * (alpha + beta * start),
                wb + vb * beta * wf * scale,
            )
            alphas.append(alpha)
            betas.append(beta)
        after = jnp.zeros((8, 128), f32)
        f_ref[blocks, tile] = after
        b_ref[0, tile] = after
        for g in range(blocks - 1, -1, -1):
            b_ref[g + 1, tile] = alphas[g] + betas[g] * after
            after = starts[g] + scales[g] * after
            f_ref[g, tile] = after
    for pair in range(4):
        for copy in copies[pair]:
            copy.wait()
        if pair == 0:
            table.wait()
        columns = []
        for tile in range(tiles):
            both = []
            for p in range(2):
                mode = 2 * pair + p
                part = slice(mode * 128, (mode + 1) * 128)
                left = b_ref[me, tile, pl.ds(mode, 1), :]
                right = f_ref[me + 1, tile, pl.ds(mode, 1), :]
                both.append(
                    y_ref[tile, part, :] + v[tile, part, :] * left + w[tile, part, :] * right
                )
            columns.append(jnp.concatenate(both, axis=0))
        half = tiles // 2
        y = to_nodes(
            *(
                lax.dot_general(
                    t[k],
                    parts(jnp.concatenate(columns[k * half : (k + 1) * half], axis=1), 1),
                    (((1,), (1,)), ((), ())),
                    preferred_element_type=f32,
                )
                for k in range(2)
            )
        )
        for p in range(2):
            part = y[:, 128 * p : 128 * (p + 1)]
            o_ref[:, 2 * pair + p] = part.reshape(part.shape[0] // 8, 8, 128)


def flow_inverse_kernel(x_ref, t_ref, o_hbm, o, sems):
    slots = x_ref.shape[0] // 8
    half = slots // 2
    stores = []
    for pair in range(4):
        plane = 2 * pair
        x = jnp.concatenate([x_ref[pl.ds(plane + p, slots, stride=8), :] for p in range(2)], axis=1)
        y = to_nodes(*(dot(t_ref[k], parts(x[k * half : (k + 1) * half], 0)) for k in range(2)))
        for p in range(2):
            o[plane + p] = y[:, 128 * p : 128 * (p + 1)]
        part = pl.ds(plane, 2)
        stores.append(pltpu.make_async_copy(o.at[part], o_hbm.at[part], sems.at[pair]))
        stores[-1].start()
    for copy in stores:
        copy.wait()


def local(velocity, spacing):
    planes, flow_length, rows = velocity.shape[1:]
    size_x = lax.axis_size("gx")
    size_z = lax.axis_size("gz")
    blocks = lax.axis_size("gy")
    group = size_x * size_z
    span_length = planes * group
    modes = flow_length // group
    tiles = span_length // 128
    flow_forward, flow_derive, flow_inverse, flow_square = np_tables(flow_length, 1.0)
    span_forward, span_derive, span_inverse, span_square = np_tables(span_length, span_step)
    field_flops = 2 * 3 * planes * rows * flow_length * flow_length
    field_bytes = 4 * planes * rows * flow_length
    me = lax.axis_index("gy")
    both = ("gx", "gz")

    def moved(x):
        return lax.all_to_all(x, both, split_axis=0, concat_axis=0, tiled=True)

    field_shape = jax.ShapeDtypeStruct((group, planes, modes, rows), f32)
    table = jnp.asarray(slots_left(flow_forward))
    plane_block = lambda c: pl.BlockSpec((1, 2, flow_length, rows), lambda i: (c, i, 0, 0))
    whole = lambda *shape: pl.BlockSpec(shape, lambda i: (0,) * len(shape))
    out_block = pl.BlockSpec((group, 2, modes, rows), lambda i: (0, i, 0, 0))
    any_place = pl.BlockSpec(memory_space=pl.ANY)
    span_sent = pl.pallas_call(
        span_field_kernel,
        in_specs=[any_place] * 2,
        out_specs=any_place,
        out_shape=field_shape,
        scratch_shapes=[
            pltpu.VMEM((planes, flow_length, rows), f32),
            pltpu.VMEM(table.shape, bf16),
            pltpu.VMEM(field_shape.shape, f32),
            pltpu.SemaphoreType.DMA((10,)),
        ],
        compiler_params=params(58),
        cost_estimate=cost(field_flops, 2 * field_bytes),
        name="span_field",
    )(velocity, table)
    span_here = moved(span_sent)

    v = velocity[1]
    up = [(i, i + 1) for i in range(blocks - 1)]
    down = [(j, i) for i, j in up]
    before = lax.ppermute(v[:, :, rows - 1], "gy", up)
    after = lax.ppermute(v[:, :, 0], "gy", down)
    gaps = lax.dynamic_slice_in_dim(spacing, me * rows, rows + 1)
    width = gaps[:-1] + gaps[1:]
    lower = 2.0 / (width * gaps[:-1])
    upper = 2.0 / (width * gaps[1:])
    flow_table = jnp.asarray(
        np.concatenate([slots_left(flow_derive), slots_left(flow_forward)], axis=2)
    )
    flow_sent = pl.pallas_call(
        flow_field_kernel,
        grid=(planes // 2,),
        in_specs=[
            plane_block(0),
            plane_block(1),
            whole(planes, flow_length),
            whole(planes, flow_length),
            whole(1, rows),
            whole(*flow_table.shape),
        ],
        out_specs=out_block,
        out_shape=field_shape,
        compiler_params=params(58),
        cost_estimate=cost(2 * field_flops, 3 * field_bytes),
        name="flow_field",
    )(velocity, velocity, before, after, width.reshape(1, rows), flow_table)
    flow_here = moved(flow_sent)

    first_mode = (lax.axis_index("gx") * size_z + lax.axis_index("gz")) * modes
    mode_square = lax.dynamic_slice_in_dim(jnp.asarray(flow_square), first_mode, modes)
    sigma = mode_square[None, :, None] + jnp.asarray(span_square).reshape(tiles, 1, 128)
    step_shape = jax.ShapeDtypeStruct((rows, tiles, modes, 128), f32)
    slab_shape = jax.ShapeDtypeStruct((tiles, modes * rows, 128), f32)
    vmem = pl.BlockSpec(memory_space=pltpu.VMEM)
    smem = pl.BlockSpec(memory_space=pltpu.SMEM)
    inv, v_all, w_all, vw_ends = pl.pallas_call(
        factor_kernel,
        in_specs=[smem, smem, vmem],
        out_specs=[vmem] * 4,
        out_shape=[step_shape]
        + [slab_shape] * 2
        + [jax.ShapeDtypeStruct((4, tiles, modes, 128), f32)],
        compiler_params=params(58),
        cost_estimate=cost(field_flops, 3 * field_bytes),
        name="factor",
    )(lower, upper, sigma)
    rings = [[(i, (i + n) % blocks) for i in range(blocks)] for n in range(1, blocks)]
    vw = jnp.stack([vw_ends] + [lax.ppermute(vw_ends, "gy", ring) for ring in rings])
    weight = jnp.broadcast_to((0.5 * width)[:, None], (rows, 128))
    end_gaps = jnp.stack([gaps[0], gaps[rows]])
    span_here, vw, weight, end_gaps = lax.optimization_barrier((span_here, vw, weight, end_gaps))

    flat = (span_length * modes, rows)
    hbm = pl.BlockSpec(memory_space=pltpu.HBM)
    span_source = pl.pallas_call(
        span_first_kernel,
        in_specs=[vmem, vmem],
        out_specs=vmem,
        out_shape=slab_shape,
        compiler_params=params(58),
        cost_estimate=cost(field_flops, 2 * field_bytes),
        name="span_first",
    )(span_here.reshape(flat), jnp.asarray(slots_right(span_derive)))
    slab = pltpu.VMEM(slab_shape.shape, f32)
    source, y_ends = pl.pallas_call(
        source_kernel,
        in_specs=[vmem, vmem, smem] + [hbm] * 4,
        out_specs=[vmem] * 2,
        out_shape=[slab_shape, jax.ShapeDtypeStruct((2, tiles, modes, 128), f32)],
        scratch_shapes=[
            pltpu.VMEM((2, 3 * span_length // 2, span_length // 2), bf16),
            slab,
            slab,
            slab,
            pltpu.SemaphoreType.DMA((13,)),
        ],
        compiler_params=params(48),
        cost_estimate=cost(field_flops, 5 * field_bytes),
        name="source",
    )(
        flow_here.reshape(flat),
        weight,
        end_gaps,
        jnp.asarray(slots_right(span_forward)),
        span_source,
        v_all,
        w_all,
    )
    ends = [y_ends] + [lax.ppermute(y_ends, "gy", ring) for ring in rings]
    step = pltpu.VMEM(step_shape.shape, f32)
    y_all = pl.pallas_call(
        sweep_kernel,
        in_specs=[smem, smem, vmem, hbm],
        out_specs=vmem,
        out_shape=slab_shape,
        scratch_shapes=[step] * 2 + [pltpu.SemaphoreType.DMA((4,))],
        compiler_params=params(32),
        cost_estimate=cost(field_flops, 3 * field_bytes),
        name="sweep",
    )(lower, upper, source, inv)
    end_shape = (blocks + 1, tiles, modes, 128)
    back_sent = pl.pallas_call(
        join_kernel,
        in_specs=[smem] + [vmem] * (2 + blocks) + [hbm] * 3,
        out_specs=vmem,
        out_shape=jax.ShapeDtypeStruct((group, modes, planes, rows), f32),
        scratch_shapes=[
            pltpu.VMEM((blocks, 2, tiles, modes, 128), f32),
            pltpu.VMEM(end_shape, f32),
            pltpu.VMEM(end_shape, f32),
            slab,
            slab,
            pltpu.VMEM((2, span_length // 2, 3 * span_length // 2), bf16),
            pltpu.SemaphoreType.DMA((9,)),
        ],
        compiler_params=params(32),
        cost_estimate=cost(field_flops, 4 * field_bytes),
        name="join",
    )(
        me.reshape(1).astype(jnp.int32),
        y_all,
        *ends,
        vw,
        v_all,
        w_all,
        jnp.asarray(nodes_left(span_inverse)),
    )
    back_here = moved(back_sent)
    last_table = jnp.asarray(nodes_left(flow_inverse))
    return pl.pallas_call(
        flow_inverse_kernel,
        in_specs=[vmem] * 2,
        out_specs=any_place,
        out_shape=jax.ShapeDtypeStruct((planes, flow_length, rows), f32),
        scratch_shapes=[
            pltpu.VMEM((planes, flow_length, rows), f32),
            pltpu.SemaphoreType.DMA((4,)),
        ],
        compiler_params=params(32),
        cost_estimate=cost(field_flops, 2 * field_bytes),
        name="flow_inverse",
    )(back_here.reshape(flow_length * planes, rows), last_table)


def solution(mesh):
    return jax.shard_map(
        local,
        mesh=mesh,
        in_specs=(P(None, ("gx", "gz"), None, "gy"), P()),
        out_specs=P(("gx", "gz"), None, "gy"),
        check_vma=False,
    )
```

```python
import functools
import math

import jax
import jax.numpy as jnp
import ml_dtypes
import numpy as np
from jax import lax
from jax.experimental import pallas as pl
from jax.experimental.pallas import tpu as pltpu
from jax.sharding import PartitionSpec as P

span_step = 0.5
f32 = jnp.float32
bf16 = jnp.bfloat16


def np_tables(length, step_size):
    index = np.arange(length)
    wave = np.where(index == 1, length // 2, index // 2)
    phase = (index[:, None] * wave[None, :]) % length
    angle = 2.0 * math.pi / length * phase
    odd_high = np.logical_and(index % 2 == 1, index >= 3)[None, :]
    forward = np.where(odd_high, -np.sin(angle), np.cos(angle))
    kappa = 2.0 * math.pi / (length * step_size) * wave
    scale = np.where(index >= 2, kappa, 0.0)[None, :]
    derive = np.where(odd_high, np.cos(angle), np.sin(angle)) * scale
    weight = np.where(index >= 2, 2.0, 1.0) / length
    inverse = forward * weight[None, :]
    order = np.argsort(wave % 2, kind="stable")
    square = (kappa * kappa).astype(np.float32)
    return forward[:, order], derive[:, order], inverse[:, order], square[order]


def halved(table):
    half = table.shape[0] // 2
    return table[:half, :half], table[:half, half:]


def split_np(table):
    high = table.astype(np.float32).astype(ml_dtypes.bfloat16)
    low = (table - high.astype(np.float64)).astype(np.float32).astype(ml_dtypes.bfloat16)
    return high, low


def thrice(table, axis):
    high, low = split_np(table)
    return np.concatenate([high, low, high], axis=axis)


def slots_left(table):
    return np.stack([thrice(part.T, 1) for part in halved(table)])


def slots_right(table):
    return np.stack([thrice(part, 0) for part in halved(table)])


def nodes_left(table):
    return np.stack([thrice(part, 1) for part in halved(table)])


def parts(x, axis):
    high = x.astype(bf16)
    low = (x - high.astype(f32)).astype(bf16)
    return jnp.concatenate([high, high, low], axis=axis)


def folded(x, axis):
    half = x.shape[axis] // 2
    first = lax.slice_in_dim(x, 0, half, axis=axis)
    second = lax.slice_in_dim(x, half, 2 * half, axis=axis)
    return parts(first + second, axis), parts(first - second, axis)


def to_nodes(even, odd):
    return jnp.concatenate([even + odd, even - odd], axis=0)


def dot(a, b):
    return jnp.dot(a, b, preferred_element_type=f32)


def params(mib):
    return pltpu.CompilerParams(vmem_limit_bytes=mib * 1024 * 1024)


def cost(flops, size):
    return pl.CostEstimate(flops=flops, bytes_accessed=size, transcendentals=0)


def span_field_kernel(w_hbm, t_hbm, o_hbm, w, t, o, sems):
    loads, stores = [], []
    for pair in range(4):
        part = pl.ds(2 * pair, 2)
        loads.append(pltpu.make_async_copy(w_hbm.at[2, part], w.at[part], sems.at[pair]))
        stores.append(pltpu.make_async_copy(o.at[:, part], o_hbm.at[:, part], sems.at[4 + pair]))
    tables = [pltpu.make_async_copy(t_hbm.at[k], t.at[k], sems.at[8 + k]) for k in range(2)]
    loads[0].start()
    for copy in tables + loads[1:]:
        copy.start()
    for pair in range(4):
        loads[pair].wait()
        x = jnp.concatenate([w[2 * pair], w[2 * pair + 1]], axis=1)
        for k, part in enumerate(folded(x, 0)):
            if pair == 0:
                tables[k].wait()
            store_modes(o.at[:, 2 * pair : 2 * pair + 2], k, dot(t[k], part))
        stores[pair].start()
    for copy in stores:
        copy.wait()


def store_modes(o_ref, k, y):
    owners = y.shape[0] // 8
    for p in range(2):
        part = y[:, 128 * p : 128 * (p + 1)].reshape(owners, 8, 128)
        o_ref[k * owners : (k + 1) * owners, p] = part


def flow_field_kernel(u_ref, v_ref, before_ref, after_ref, width_ref, t_ref, o_ref):
    step = pl.program_id(0)
    lane = lax.broadcasted_iota(jnp.int32, v_ref.shape[2:], 1)
    width = width_ref[...]
    slopes = []
    for p in range(2):
        v = v_ref[0, p]
        z = step * 2 + p
        before = jnp.transpose(jnp.broadcast_to(before_ref[pl.ds(z, 1), :], (128, v.shape[0])))
        after = jnp.transpose(jnp.broadcast_to(after_ref[pl.ds(z, 1), :], (128, v.shape[0])))
        down = jnp.where(lane == 0, before, pltpu.roll(v, 1, 1))
        up = jnp.where(lane == 127, after, pltpu.roll(v, 127, 1))
        slopes.append((up - down) / width)
    u = jnp.concatenate([u_ref[0, 0], u_ref[0, 1]], axis=1)
    s = jnp.concatenate(slopes, axis=1)
    for k, pair in enumerate(zip(folded(u, 0), folded(s, 0))):
        store_modes(o_ref, k, dot(t_ref[k], jnp.concatenate(pair, axis=0)))


def factor_kernel(low_ref, up_ref, sigma_ref, inv_ref, v_ref, w_ref, ends_ref):
    rows = inv_ref.shape[0]
    tiles = inv_ref.shape[1]

    def ahead(y, carry):
        low = low_ref[y]
        up = up_ref[y]
        out = []
        for t in range(tiles):
            r, val = carry[t]
            inv = 1.0 / (-(low + up) - sigma_ref[t] - low * r)
            val = -(low * inv) * val
            inv_ref[y, t] = inv
            v_ref[t, pl.ds(y, 8, stride=rows), :] = val
            out.append((up * inv, val))
        return tuple(out)

    zero = jnp.zeros((8, 128), f32)
    one = jnp.ones((8, 128), f32)
    lax.fori_loop(0, rows, ahead, ((zero, one),) * tiles)

    def back(s, carry):
        y = rows - 1 - s
        out = []
        for t in range(tiles):
            v, w = carry[t]
            r = up_ref[y] * inv_ref[y, t]
            v = v_ref[t, pl.ds(y, 8, stride=rows), :] - r * v
            w = -r * w
            v_ref[t, pl.ds(y, 8, stride=rows), :] = v
            w_ref[t, pl.ds(y, 8, stride=rows), :] = w
            out.append((v, w))
        return tuple(out)

    first = lax.fori_loop(0, rows, back, ((zero, one),) * tiles)
    for t in range(tiles):
        ends_ref[0, t] = first[t][0]
        ends_ref[1, t] = v_ref[t, pl.ds(rows - 1, 8, stride=rows), :]
        ends_ref[2, t] = first[t][1]
        ends_ref[3, t] = w_ref[t, pl.ds(rows - 1, 8, stride=rows), :]


def span_sides(x_ref, mode, count):
    planes = x_ref.shape[0] // 8
    some = [
        jnp.transpose(x_ref[pl.ds(mode + p, planes, stride=8), :]) for p in range(count)
    ]
    return folded(jnp.concatenate(some, axis=0), 1)


def span_modes(sides, t_ref):
    return jnp.concatenate([dot(part, t_ref[k]) for k, part in enumerate(sides)], axis=1)


def span_first_kernel(x_ref, t_ref, o_ref):
    tiles = o_ref.shape[0]
    for mode in range(0, 8, 2):
        y = span_modes(span_sides(x_ref, mode, 2), t_ref)
        for t in range(tiles):
            o_ref[t, mode * 128 : (mode + 2) * 128, :] = y[:, t * 128 : (t + 1) * 128]


def pair_copies(hbm, held, sems, first):
    out = []
    for pair in range(4):
        part = pl.ds(pair * 256, 256)
        out.append(
            pltpu.make_async_copy(hbm.at[:, part, :], held.at[:, part, :], sems.at[first + pair])
        )
    return out


def source_kernel(
    x_ref, weight_ref, gap_ref, t_hbm, s_hbm, v_hbm, w_hbm, o_ref, ends_ref, t, s, v, w, sems
):
    tiles = o_ref.shape[0]
    table = pltpu.make_async_copy(t_hbm, t, sems.at[0])
    table.start()
    copies = list(
        zip(
            pair_copies(s_hbm, s, sems, 1),
            pair_copies(v_hbm, v, sems, 5),
            pair_copies(w_hbm, w, sems, 9),
        )
    )
    for group in copies:
        for copy in group:
            copy.start()
    weight = weight_ref[...]
    for pair in range(4):
        if pair % 2 == 0:
            sides = span_sides(x_ref, 2 * pair, 4)
            if pair == 0:
                table.wait()
            four = span_modes(sides, t)
        y = four[pair % 2 * 256 : (pair % 2 + 1) * 256]
        for copy in copies[pair]:
            copy.wait()
        for p in range(2):
            mode = 2 * pair + p
            part = slice(mode * 128, (mode + 1) * 128)
            for tile in range(tiles):
                side = y[p * 128 : (p + 1) * 128, tile * 128 : (tile + 1) * 128] + s[tile, part, :]
                o_ref[tile, part, :] = side
                side = side * weight
                row = slice(mode, mode + 1)
                ends_ref[0, tile, row, :] = -gap_ref[0] * jnp.sum(
                    side * v[tile, part, :], axis=0, keepdims=True
                )
                ends_ref[1, tile, row, :] = -gap_ref[1] * jnp.sum(
                    side * w[tile, part, :], axis=0, keepdims=True
                )


def sweep_kernel(low_ref, up_ref, x_ref, inv_hbm, o_ref, inv, held, sems):
    tiles = o_ref.shape[0]
    rows = inv.shape[0]
    count = 4
    chunk = rows // count
    copies = [
        pltpu.make_async_copy(
            inv_hbm.at[pl.ds(c * chunk, chunk)], inv.at[pl.ds(c * chunk, chunk)], sems.at[c]
        )
        for c in range(count)
    ]
    for copy in copies:
        copy.start()

    def ahead(block, carry):
        for j in range(8):
            y = block * 8 + j
            low = low_ref[y]
            out = []
            for t in range(tiles):
                scale = inv[y, t]
                side = x_ref[t, pl.ds(y, 8, stride=rows), :]
                val = side * scale - (low * scale) * carry[t]
                held[y, t] = val
                out.append(val)
            carry = tuple(out)
        return carry

    carry = (jnp.zeros((8, 128), f32),) * tiles
    for c in range(count):
        copies[c].wait()
        carry = lax.fori_loop(c * chunk // 8, (c + 1) * chunk // 8, ahead, carry)

    def back(step, carry):
        for j in range(8):
            y = rows - 1 - (step * 8 + j)
            up = up_ref[y]
            out = []
            for t in range(tiles):
                val = held[y, t] - (up * inv[y, t]) * carry[t]
                o_ref[t, pl.ds(y, 8, stride=rows), :] = val
                out.append(val)
            carry = tuple(out)
        return carry

    lax.fori_loop(0, rows // 8, back, (jnp.zeros((8, 128), f32),) * tiles)


def join_kernel(me_ref, y_ref, *refs):
    ends, (vw_ref, v_hbm, w_hbm, t_hbm, o_ref, ys_ref, b_ref, f_ref, v, w, t, sems) = (
        refs[:-12],
        refs[-12:],
    )
    blocks = vw_ref.shape[0]
    tiles = y_ref.shape[0]
    me = me_ref[0]
    table = pltpu.make_async_copy(t_hbm, t, sems.at[0])
    copies = list(zip(pair_copies(v_hbm, v, sems, 1), pair_copies(w_hbm, w, sems, 5)))
    for copy in copies[0]:
        copy.start()
    table.start()
    for group in copies[1:]:
        for copy in group:
            copy.start()
    for shift in range(blocks):
        ys_ref[shift] = ends[shift][...]
    for tile in range(tiles):
        alpha = jnp.zeros((8, 128), f32)
        beta = jnp.zeros((8, 128), f32)
        alphas, betas, starts, scales = [], [], [], []
        for g in range(blocks):
            slot = lax.rem(me + blocks - g, blocks)
            yf = ys_ref[slot, 0, tile]
            yb = ys_ref[slot, 1, tile]
            vf, vb, wf, wb = (vw_ref[slot, n, tile] for n in range(4))
            scale = 1.0 / (1.0 - vf * beta)
            start = (yf + vf * alpha) * scale
            starts.append(start)
            scales.append(wf * scale)
            alpha, beta = (
                yb + vb * (alpha + beta * start),
                wb + vb * beta * wf * scale,
            )
            alphas.append(alpha)
            betas.append(beta)
        after = jnp.zeros((8, 128), f32)
        f_ref[blocks, tile] = after
        b_ref[0, tile] = after
        for g in range(blocks - 1, -1, -1):
            b_ref[g + 1, tile] = alphas[g] + betas[g] * after
            after = starts[g] + scales[g] * after
            f_ref[g, tile] = after
    for pair in range(4):
        for copy in copies[pair]:
            copy.wait()
        if pair == 0:
            table.wait()
        columns = []
        for tile in range(tiles):
            both = []
            for p in range(2):
                mode = 2 * pair + p
                part = slice(mode * 128, (mode + 1) * 128)
                left = b_ref[me, tile, pl.ds(mode, 1), :]
                right = f_ref[me + 1, tile, pl.ds(mode, 1), :]
                both.append(
                    y_ref[tile, part, :] + v[tile, part, :] * left + w[tile, part, :] * right
                )
            columns.append(jnp.concatenate(both, axis=0))
        half = tiles // 2
        y = to_nodes(
            *(
                lax.dot_general(
                    t[k],
                    parts(jnp.concatenate(columns[k * half : (k + 1) * half], axis=1), 1),
                    (((1,), (1,)), ((), ())),
                    preferred_element_type=f32,
                )
                for k in range(2)
            )
        )
        for p in range(2):
            part = y[:, 128 * p : 128 * (p + 1)]
            o_ref[:, 2 * pair + p] = part.reshape(part.shape[0] // 8, 8, 128)


def flow_inverse_kernel(x_ref, t_ref, o_hbm, o, sems):
    slots = x_ref.shape[0] // 8
    half = slots // 2
    stores = []
    for pair in range(4):
        plane = 2 * pair
        x = jnp.concatenate([x_ref[pl.ds(plane + p, slots, stride=8), :] for p in range(2)], axis=1)
        y = to_nodes(*(dot(t_ref[k], parts(x[k * half : (k + 1) * half], 0)) for k in range(2)))
        for p in range(2):
            o[plane + p] = y[:, 128 * p : 128 * (p + 1)]
        part = pl.ds(plane, 2)
        stores.append(pltpu.make_async_copy(o.at[part], o_hbm.at[part], sems.at[pair]))
        stores[-1].start()
    for copy in stores:
        copy.wait()


def local(velocity, spacing):
    planes, flow_length, rows = velocity.shape[1:]
    size_x = lax.axis_size("gx")
    size_z = lax.axis_size("gz")
    blocks = lax.axis_size("gy")
    group = size_x * size_z
    span_length = planes * group
    modes = flow_length // group
    tiles = span_length // 128
    flow_forward, flow_derive, flow_inverse, flow_square = np_tables(flow_length, 1.0)
    span_forward, span_derive, span_inverse, span_square = np_tables(span_length, span_step)
    field_flops = 2 * 3 * planes * rows * flow_length * flow_length
    field_bytes = 4 * planes * rows * flow_length
    me = lax.axis_index("gy")
    both = ("gx", "gz")

    def moved(x):
        return lax.all_to_all(x, both, split_axis=0, concat_axis=0, tiled=True)

    field_shape = jax.ShapeDtypeStruct((group, planes, modes, rows), f32)
    table = jnp.asarray(slots_left(flow_forward))
    plane_block = lambda c: pl.BlockSpec((1, 2, flow_length, rows), lambda i: (c, i, 0, 0))
    whole = lambda *shape: pl.BlockSpec(shape, lambda i: (0,) * len(shape))
    out_block = pl.BlockSpec((group, 2, modes, rows), lambda i: (0, i, 0, 0))
    any_place = pl.BlockSpec(memory_space=pl.ANY)
    span_sent = pl.pallas_call(
        span_field_kernel,
        in_specs=[any_place] * 2,
        out_specs=any_place,
        out_shape=field_shape,
        scratch_shapes=[
            pltpu.VMEM((planes, flow_length, rows), f32),
            pltpu.VMEM(table.shape, bf16),
            pltpu.VMEM(field_shape.shape, f32),
            pltpu.SemaphoreType.DMA((10,)),
        ],
        compiler_params=params(58),
        cost_estimate=cost(field_flops, 2 * field_bytes),
        name="span_field",
    )(velocity, table)
    span_here = moved(span_sent)

    v = velocity[1]
    up = [(i, i + 1) for i in range(blocks - 1)]
    down = [(j, i) for i, j in up]
    before = lax.ppermute(v[:, :, rows - 1], "gy", up)
    after = lax.ppermute(v[:, :, 0], "gy", down)
    gaps = lax.dynamic_slice_in_dim(spacing, me * rows, rows + 1)
    width = gaps[:-1] + gaps[1:]
    lower = 2.0 / (width * gaps[:-1])
    upper = 2.0 / (width * gaps[1:])
    flow_table = jnp.asarray(
        np.concatenate([slots_left(flow_derive), slots_left(flow_forward)], axis=2)
    )
    flow_sent = pl.pallas_call(
        flow_field_kernel,
        grid=(planes // 2,),
        in_specs=[
            plane_block(0),
            plane_block(1),
            whole(planes, flow_length),
            whole(planes, flow_length),
            whole(1, rows),
            whole(*flow_table.shape),
        ],
        out_specs=out_block,
        out_shape=field_shape,
        compiler_params=params(58),
        cost_estimate=cost(2 * field_flops, 3 * field_bytes),
        name="flow_field",
    )(velocity, velocity, before, after, width.reshape(1, rows), flow_table)
    flow_here = moved(flow_sent)

    first_mode = (lax.axis_index("gx") * size_z + lax.axis_index("gz")) * modes
    mode_square = lax.dynamic_slice_in_dim(jnp.asarray(flow_square), first_mode, modes)
    sigma = mode_square[None, :, None] + jnp.asarray(span_square).reshape(tiles, 1, 128)
    step_shape = jax.ShapeDtypeStruct((rows, tiles, modes, 128), f32)
    slab_shape = jax.ShapeDtypeStruct((tiles, modes * rows, 128), f32)
    vmem = pl.BlockSpec(memory_space=pltpu.VMEM)
    smem = pl.BlockSpec(memory_space=pltpu.SMEM)
    inv, v_all, w_all, vw_ends = pl.pallas_call(
        factor_kernel,
        in_specs=[smem, smem, vmem],
        out_specs=[vmem] * 4,
        out_shape=[step_shape]
        + [slab_shape] * 2
        + [jax.ShapeDtypeStruct((4, tiles, modes, 128), f32)],
        compiler_params=params(58),
        cost_estimate=cost(field_flops, 3 * field_bytes),
        name="factor",
    )(lower, upper, sigma)
    rings = [[(i, (i + n) % blocks) for i in range(blocks)] for n in range(1, blocks)]
    vw = jnp.stack([vw_ends] + [lax.ppermute(vw_ends, "gy", ring) for ring in rings])
    weight = jnp.broadcast_to((0.5 * width)[:, None], (rows, 128))
    end_gaps = jnp.stack([gaps[0], gaps[rows]])
    span_here, vw, weight, end_gaps = lax.optimization_barrier((span_here, vw, weight, end_gaps))

    flat = (span_length * modes, rows)
    hbm = pl.BlockSpec(memory_space=pltpu.HBM)
    span_source = pl.pallas_call(
        span_first_kernel,
        in_specs=[vmem, vmem],
        out_specs=vmem,
        out_shape=slab_shape,
        compiler_params=params(58),
        cost_estimate=cost(field_flops, 2 * field_bytes),
        name="span_first",
    )(span_here.reshape(flat), jnp.asarray(slots_right(span_derive)))
    slab = pltpu.VMEM(slab_shape.shape, f32)
    source, y_ends = pl.pallas_call(
        source_kernel,
        in_specs=[vmem, vmem, smem] + [hbm] * 4,
        out_specs=[vmem] * 2,
        out_shape=[slab_shape, jax.ShapeDtypeStruct((2, tiles, modes, 128), f32)],
        scratch_shapes=[
            pltpu.VMEM((2, 3 * span_length // 2, span_length // 2), bf16),
            slab,
            slab,
            slab,
            pltpu.SemaphoreType.DMA((13,)),
        ],
        compiler_params=params(48),
        cost_estimate=cost(field_flops, 5 * field_bytes),
        name="source",
    )(
        flow_here.reshape(flat),
        weight,
        end_gaps,
        jnp.asarray(slots_right(span_forward)),
        span_source,
        v_all,
        w_all,
    )
    ends = [y_ends] + [lax.ppermute(y_ends, "gy", ring) for ring in rings]
    step = pltpu.VMEM(step_shape.shape, f32)
    y_all = pl.pallas_call(
        sweep_kernel,
        in_specs=[smem, smem, vmem, hbm],
        out_specs=vmem,
        out_shape=slab_shape,
        scratch_shapes=[step] * 2 + [pltpu.SemaphoreType.DMA((4,))],
        compiler_params=params(32),
        cost_estimate=cost(field_flops, 3 * field_bytes),
        name="sweep",
    )(lower, upper, source, inv)
    end_shape = (blocks + 1, tiles, modes, 128)
    back_sent = pl.pallas_call(
        join_kernel,
        in_specs=[smem] + [vmem] * (2 + blocks) + [hbm] * 3,
        out_specs=vmem,
        out_shape=jax.ShapeDtypeStruct((group, modes, planes, rows), f32),
        scratch_shapes=[
            pltpu.VMEM((blocks, 2, tiles, modes, 128), f32),
            pltpu.VMEM(end_shape, f32),
            pltpu.VMEM(end_shape, f32),
            slab,
            slab,
            pltpu.VMEM((2, span_length // 2, 3 * span_length // 2), bf16),
            pltpu.SemaphoreType.DMA((9,)),
        ],
        compiler_params=params(32),
        cost_estimate=cost(field_flops, 4 * field_bytes),
        name="join",
    )(
        me.reshape(1).astype(jnp.int32),
        y_all,
        *ends,
        vw,
        v_all,
        w_all,
        jnp.asarray(nodes_left(span_inverse)),
    )
    back_here = moved(back_sent)
    last_table = jnp.asarray(nodes_left(flow_inverse))
    return pl.pallas_call(
        flow_inverse_kernel,
        in_specs=[vmem] * 2,
        out_specs=any_place,
        out_shape=jax.ShapeDtypeStruct((planes, flow_length, rows), f32),
        scratch_shapes=[
            pltpu.VMEM((planes, flow_length, rows), f32),
            pltpu.SemaphoreType.DMA((4,)),
        ],
        compiler_params=params(32),
        cost_estimate=cost(field_flops, 2 * field_bytes),
        name="flow_inverse",
    )(back_here.reshape(flow_length * planes, rows), last_table)


def solution(mesh):
    return jax.shard_map(
        local,
        mesh=mesh,
        in_specs=(P(None, ("gx", "gz"), None, "gy"), P()),
        out_specs=P(("gx", "gz"), None, "gy"),
        check_vma=False,
    )
```

```python
import functools
import math

import jax
import jax.numpy as jnp
import ml_dtypes
import numpy as np
from jax import lax
from jax.experimental import pallas as pl
from jax.experimental.pallas import tpu as pltpu
from jax.sharding import PartitionSpec as P

span_step = 0.5
f32 = jnp.float32
bf16 = jnp.bfloat16


def np_tables(length, step_size):
    index = np.arange(length)
    wave = np.where(index == 1, length // 2, index // 2)
    phase = (index[:, None] * wave[None, :]) % length
    angle = 2.0 * math.pi / length * phase
    odd_high = np.logical_and(index % 2 == 1, index >= 3)[None, :]
    forward = np.where(odd_high, -np.sin(angle), np.cos(angle))
    kappa = 2.0 * math.pi / (length * step_size) * wave
    scale = np.where(index >= 2, kappa, 0.0)[None, :]
    derive = np.where(odd_high, np.cos(angle), np.sin(angle)) * scale
    weight = np.where(index >= 2, 2.0, 1.0) / length
    inverse = forward * weight[None, :]
    order = np.argsort(wave % 2, kind="stable")
    square = (kappa * kappa).astype(np.float32)
    return forward[:, order], derive[:, order], inverse[:, order], square[order]


def halved(table):
    half = table.shape[0] // 2
    return table[:half, :half], table[:half, half:]


def split_np(table):
    high = table.astype(np.float32).astype(ml_dtypes.bfloat16)
    low = (table - high.astype(np.float64)).astype(np.float32).astype(ml_dtypes.bfloat16)
    return high, low


def thrice(table, axis):
    high, low = split_np(table)
    return np.concatenate([high, low, high], axis=axis)


def slots_left(table):
    return np.stack([thrice(part.T, 1) for part in halved(table)])


def slots_right(table):
    return np.stack([thrice(part, 0) for part in halved(table)])


def nodes_left(table):
    return np.stack([thrice(part, 1) for part in halved(table)])


def parts(x, axis):
    high = x.astype(bf16)
    low = (x - high.astype(f32)).astype(bf16)
    return jnp.concatenate([high, high, low], axis=axis)


def folded(x, axis):
    half = x.shape[axis] // 2
    first = lax.slice_in_dim(x, 0, half, axis=axis)
    second = lax.slice_in_dim(x, half, 2 * half, axis=axis)
    return parts(first + second, axis), parts(first - second, axis)


def to_nodes(even, odd):
    return jnp.concatenate([even + odd, even - odd], axis=0)


def dot(a, b):
    return jnp.dot(a, b, preferred_element_type=f32)


def params(mib):
    return pltpu.CompilerParams(vmem_limit_bytes=mib * 1024 * 1024)


def cost(flops, size):
    return pl.CostEstimate(flops=flops, bytes_accessed=size, transcendentals=0)


def span_field_kernel(w_hbm, t_hbm, o_hbm, w, t, o, sems):
    loads, stores = [], []
    for pair in range(4):
        part = pl.ds(2 * pair, 2)
        loads.append(pltpu.make_async_copy(w_hbm.at[2, part], w.at[part], sems.at[pair]))
        stores.append(pltpu.make_async_copy(o.at[:, part], o_hbm.at[:, part], sems.at[4 + pair]))
    tables = [pltpu.make_async_copy(t_hbm.at[k], t.at[k], sems.at[8 + k]) for k in range(2)]
    loads[0].start()
    for copy in tables + loads[1:]:
        copy.start()
    for pair in range(4):
        loads[pair].wait()
        x = jnp.concatenate([w[2 * pair], w[2 * pair + 1]], axis=1)
        for k, part in enumerate(folded(x, 0)):
            if pair == 0:
                tables[k].wait()
            store_modes(o.at[:, 2 * pair : 2 * pair + 2], k, dot(t[k], part))
        stores[pair].start()
    for copy in stores:
        copy.wait()


def store_modes(o_ref, k, y):
    owners = y.shape[0] // 8
    for p in range(2):
        part = y[:, 128 * p : 128 * (p + 1)].reshape(owners, 8, 128)
        o_ref[k * owners : (k + 1) * owners, p] = part


def flow_field_kernel(u_ref, v_ref, before_ref, after_ref, width_ref, t_ref, o_ref):
    step = pl.program_id(0)
    lane = lax.broadcasted_iota(jnp.int32, v_ref.shape[2:], 1)
    width = width_ref[...]
    slopes = []
    for p in range(2):
        v = v_ref[0, p]
        z = step * 2 + p
        before = jnp.transpose(jnp.broadcast_to(before_ref[pl.ds(z, 1), :], (128, v.shape[0])))
        after = jnp.transpose(jnp.broadcast_to(after_ref[pl.ds(z, 1), :], (128, v.shape[0])))
        down = jnp.where(lane == 0, before, pltpu.roll(v, 1, 1))
        up = jnp.where(lane == 127, after, pltpu.roll(v, 127, 1))
        slopes.append((up - down) / width)
    u = jnp.concatenate([u_ref[0, 0], u_ref[0, 1]], axis=1)
    s = jnp.concatenate(slopes, axis=1)
    for k, pair in enumerate(zip(folded(u, 0), folded(s, 0))):
        store_modes(o_ref, k, dot(t_ref[k], jnp.concatenate(pair, axis=0)))


def factor_kernel(low_ref, up_ref, sigma_ref, inv_ref, v_ref, w_ref, ends_ref):
    rows = inv_ref.shape[0]
    tiles = inv_ref.shape[1]

    def ahead(y, carry):
        low = low_ref[y]
        up = up_ref[y]
        out = []
        for t in range(tiles):
            r, val = carry[t]
            inv = 1.0 / (-(low + up) - sigma_ref[t] - low * r)
            val = -(low * inv) * val
            inv_ref[y, t] = inv
            v_ref[t, pl.ds(y, 8, stride=rows), :] = val
            out.append((up * inv, val))
        return tuple(out)

    zero = jnp.zeros((8, 128), f32)
    one = jnp.ones((8, 128), f32)
    lax.fori_loop(0, rows, ahead, ((zero, one),) * tiles)

    def back(s, carry):
        y = rows - 1 - s
        out = []
        for t in range(tiles):
            v, w = carry[t]
            r = up_ref[y] * inv_ref[y, t]
            v = v_ref[t, pl.ds(y, 8, stride=rows), :] - r * v
            w = -r * w
            v_ref[t, pl.ds(y, 8, stride=rows), :] = v
            w_ref[t, pl.ds(y, 8, stride=rows), :] = w
            out.append((v, w))
        return tuple(out)

    first = lax.fori_loop(0, rows, back, ((zero, one),) * tiles)
    for t in range(tiles):
        ends_ref[0, t] = first[t][0]
        ends_ref[1, t] = v_ref[t, pl.ds(rows - 1, 8, stride=rows), :]
        ends_ref[2, t] = first[t][1]
        ends_ref[3, t] = w_ref[t, pl.ds(rows - 1, 8, stride=rows), :]


def span_sides(x_ref, mode, count):
    planes = x_ref.shape[0] // 8
    some = [
        jnp.transpose(x_ref[pl.ds(mode + p, planes, stride=8), :]) for p in range(count)
    ]
    return folded(jnp.concatenate(some, axis=0), 1)


def span_modes(sides, t_ref):
    return jnp.concatenate([dot(part, t_ref[k]) for k, part in enumerate(sides)], axis=1)


def span_first_kernel(x_ref, t_ref, o_ref):
    tiles = o_ref.shape[0]
    for mode in range(0, 8, 2):
        y = span_modes(span_sides(x_ref, mode, 2), t_ref)
        for t in range(tiles):
            o_ref[t, mode * 128 : (mode + 2) * 128, :] = y[:, t * 128 : (t + 1) * 128]


def pair_copies(hbm, held, sems, first):
    out = []
    for pair in range(4):
        part = pl.ds(pair * 256, 256)
        out.append(
            pltpu.make_async_copy(hbm.at[:, part, :], held.at[:, part, :], sems.at[first + pair])
        )
    return out


def source_kernel(
    x_ref, weight_ref, gap_ref, t_hbm, s_hbm, v_hbm, w_hbm, o_ref, ends_ref, t, s, v, w, sems
):
    tiles = o_ref.shape[0]
    table = pltpu.make_async_copy(t_hbm, t, sems.at[0])
    table.start()
    copies = list(
        zip(
            pair_copies(s_hbm, s, sems, 1),
            pair_copies(v_hbm, v, sems, 5),
            pair_copies(w_hbm, w, sems, 9),
        )
    )
    for group in copies:
        for copy in group:
            copy.start()
    weight = weight_ref[...]
    for pair in range(4):
        if pair % 2 == 0:
            sides = span_sides(x_ref, 2 * pair, 4)
            if pair == 0:
                table.wait()
            four = span_modes(sides, t)
        y = four[pair % 2 * 256 : (pair % 2 + 1) * 256]
        for copy in copies[pair]:
            copy.wait()
        for p in range(2):
            mode = 2 * pair + p
            part = slice(mode * 128, (mode + 1) * 128)
            for tile in range(tiles):
                side = y[p * 128 : (p + 1) * 128, tile * 128 : (tile + 1) * 128] + s[tile, part, :]
                o_ref[tile, part, :] = side
                side = side * weight
                row = slice(mode, mode + 1)
                ends_ref[0, tile, row, :] = -gap_ref[0] * jnp.sum(
                    side * v[tile, part, :], axis=0, keepdims=True
                )
                ends_ref[1, tile, row, :] = -gap_ref[1] * jnp.sum(
                    side * w[tile, part, :], axis=0, keepdims=True
                )


def sweep_kernel(low_ref, up_ref, x_ref, inv_hbm, o_ref, inv, held, sems):
    tiles = o_ref.shape[0]
    rows = inv.shape[0]
    count = 4
    chunk = rows // count
    copies = [
        pltpu.make_async_copy(
            inv_hbm.at[pl.ds(c * chunk, chunk)], inv.at[pl.ds(c * chunk, chunk)], sems.at[c]
        )
        for c in range(count)
    ]
    for copy in copies:
        copy.start()

    def ahead(block, carry):
        for j in range(8):
            y = block * 8 + j
            low = low_ref[y]
            out = []
            for t in range(tiles):
                scale = inv[y, t]
                side = x_ref[t, pl.ds(y, 8, stride=rows), :]
                val = side * scale - (low * scale) * carry[t]
                held[y, t] = val
                out.append(val)
            carry = tuple(out)
        return carry

    carry = (jnp.zeros((8, 128), f32),) * tiles
    for c in range(count):
        copies[c].wait()
        carry = lax.fori_loop(c * chunk // 8, (c + 1) * chunk // 8, ahead, carry)

    def back(step, carry):
        for j in range(8):
            y = rows - 1 - (step * 8 + j)
            up = up_ref[y]
            out = []
            for t in range(tiles):
                val = held[y, t] - (up * inv[y, t]) * carry[t]
                o_ref[t, pl.ds(y, 8, stride=rows), :] = val
                out.append(val)
            carry = tuple(out)
        return carry

    lax.fori_loop(0, rows // 8, back, (jnp.zeros((8, 128), f32),) * tiles)


def join_kernel(me_ref, y_ref, *refs):
    ends, (vw_ref, v_hbm, w_hbm, t_hbm, o_ref, ys_ref, b_ref, f_ref, v, w, t, sems) = (
        refs[:-12],
        refs[-12:],
    )
    blocks = vw_ref.shape[0]
    tiles = y_ref.shape[0]
    me = me_ref[0]
    table = pltpu.make_async_copy(t_hbm, t, sems.at[0])
    copies = list(zip(pair_copies(v_hbm, v, sems, 1), pair_copies(w_hbm, w, sems, 5)))
    for copy in copies[0]:
        copy.start()
    table.start()
    for group in copies[1:]:
        for copy in group:
            copy.start()
    for shift in range(blocks):
        ys_ref[shift] = ends[shift][...]
    for tile in range(tiles):
        alpha = jnp.zeros((8, 128), f32)
        beta = jnp.zeros((8, 128), f32)
        alphas, betas, starts, scales = [], [], [], []
        for g in range(blocks):
            slot = lax.rem(me + blocks - g, blocks)
            yf = ys_ref[slot, 0, tile]
            yb = ys_ref[slot, 1, tile]
            vf, vb, wf, wb = (vw_ref[slot, n, tile] for n in range(4))
            scale = 1.0 / (1.0 - vf * beta)
            start = (yf + vf * alpha) * scale
            starts.append(start)
            scales.append(wf * scale)
            alpha, beta = (
                yb + vb * (alpha + beta * start),
                wb + vb * beta * wf * scale,
            )
            alphas.append(alpha)
            betas.append(beta)
        after = jnp.zeros((8, 128), f32)
        f_ref[blocks, tile] = after
        b_ref[0, tile] = after
        for g in range(blocks - 1, -1, -1):
            b_ref[g + 1, tile] = alphas[g] + betas[g] * after
            after = starts[g] + scales[g] * after
            f_ref[g, tile] = after
    for quad in range(2):
        for copy in copies[2 * quad] + copies[2 * quad + 1]:
            copy.wait()
        columns = []
        for tile in range(tiles):
            both = []
            for p in range(4):
                mode = 4 * quad + p
                part = slice(mode * 128, (mode + 1) * 128)
                left = b_ref[me, tile, pl.ds(mode, 1), :]
                right = f_ref[me + 1, tile, pl.ds(mode, 1), :]
                both.append(
                    y_ref[tile, part, :] + v[tile, part, :] * left + w[tile, part, :] * right
                )
            columns.append(jnp.concatenate(both, axis=0))
        if quad == 0:
            table.wait()
        half = tiles // 2
        y = to_nodes(
            *(
                lax.dot_general(
                    t[k],
                    parts(jnp.concatenate(columns[k * half : (k + 1) * half], axis=1), 1),
                    (((1,), (1,)), ((), ())),
                    preferred_element_type=f32,
                )
                for k in range(2)
            )
        )
        for p in range(4):
            part = y[:, 128 * p : 128 * (p + 1)]
            o_ref[:, 4 * quad + p] = part.reshape(part.shape[0] // 8, 8, 128)


def flow_inverse_kernel(x_ref, t_ref, o_hbm, o, sems):
    slots = x_ref.shape[0] // 8
    half = slots // 2
    stores = []
    for pair in range(4):
        plane = 2 * pair
        x = jnp.concatenate([x_ref[pl.ds(plane + p, slots, stride=8), :] for p in range(2)], axis=1)
        y = to_nodes(*(dot(t_ref[k], parts(x[k * half : (k + 1) * half], 0)) for k in range(2)))
        for p in range(2):
            o[plane + p] = y[:, 128 * p : 128 * (p + 1)]
        part = pl.ds(plane, 2)
        stores.append(pltpu.make_async_copy(o.at[part], o_hbm.at[part], sems.at[pair]))
        stores[-1].start()
    for copy in stores:
        copy.wait()


def local(velocity, spacing):
    planes, flow_length, rows = velocity.shape[1:]
    size_x = lax.axis_size("gx")
    size_z = lax.axis_size("gz")
    blocks = lax.axis_size("gy")
    group = size_x * size_z
    span_length = planes * group
    modes = flow_length // group
    tiles = span_length // 128
    flow_forward, flow_derive, flow_inverse, flow_square = np_tables(flow_length, 1.0)
    span_forward, span_derive, span_inverse, span_square = np_tables(span_length, span_step)
    field_flops = 2 * 3 * planes * rows * flow_length * flow_length
    field_bytes = 4 * planes * rows * flow_length
    me = lax.axis_index("gy")
    both = ("gx", "gz")

    def moved(x):
        return lax.all_to_all(x, both, split_axis=0, concat_axis=0, tiled=True)

    field_shape = jax.ShapeDtypeStruct((group, planes, modes, rows), f32)
    table = jnp.asarray(slots_left(flow_forward))
    plane_block = lambda c: pl.BlockSpec((1, 2, flow_length, rows), lambda i: (c, i, 0, 0))
    whole = lambda *shape: pl.BlockSpec(shape, lambda i: (0,) * len(shape))
    out_block = pl.BlockSpec((group, 2, modes, rows), lambda i: (0, i, 0, 0))
    any_place = pl.BlockSpec(memory_space=pl.ANY)
    span_sent = pl.pallas_call(
        span_field_kernel,
        in_specs=[any_place] * 2,
        out_specs=any_place,
        out_shape=field_shape,
        scratch_shapes=[
            pltpu.VMEM((planes, flow_length, rows), f32),
            pltpu.VMEM(table.shape, bf16),
            pltpu.VMEM(field_shape.shape, f32),
            pltpu.SemaphoreType.DMA((10,)),
        ],
        compiler_params=params(58),
        cost_estimate=cost(field_flops, 2 * field_bytes),
        name="span_field",
    )(velocity, table)
    span_here = moved(span_sent)

    v = velocity[1]
    up = [(i, i + 1) for i in range(blocks - 1)]
    down = [(j, i) for i, j in up]
    before = lax.ppermute(v[:, :, rows - 1], "gy", up)
    after = lax.ppermute(v[:, :, 0], "gy", down)
    gaps = lax.dynamic_slice_in_dim(spacing, me * rows, rows + 1)
    width = gaps[:-1] + gaps[1:]
    lower = 2.0 / (width * gaps[:-1])
    upper = 2.0 / (width * gaps[1:])
    flow_table = jnp.asarray(
        np.concatenate([slots_left(flow_derive), slots_left(flow_forward)], axis=2)
    )
    flow_sent = pl.pallas_call(
        flow_field_kernel,
        grid=(planes // 2,),
        in_specs=[
            plane_block(0),
            plane_block(1),
            whole(planes, flow_length),
            whole(planes, flow_length),
            whole(1, rows),
            whole(*flow_table.shape),
        ],
        out_specs=out_block,
        out_shape=field_shape,
        compiler_params=params(58),
        cost_estimate=cost(2 * field_flops, 3 * field_bytes),
        name="flow_field",
    )(velocity, velocity, before, after, width.reshape(1, rows), flow_table)
    flow_here = moved(flow_sent)

    first_mode = (lax.axis_index("gx") * size_z + lax.axis_index("gz")) * modes
    mode_square = lax.dynamic_slice_in_dim(jnp.asarray(flow_square), first_mode, modes)
    sigma = mode_square[None, :, None] + jnp.asarray(span_square).reshape(tiles, 1, 128)
    step_shape = jax.ShapeDtypeStruct((rows, tiles, modes, 128), f32)
    slab_shape = jax.ShapeDtypeStruct((tiles, modes * rows, 128), f32)
    vmem = pl.BlockSpec(memory_space=pltpu.VMEM)
    smem = pl.BlockSpec(memory_space=pltpu.SMEM)
    inv, v_all, w_all, vw_ends = pl.pallas_call(
        factor_kernel,
        in_specs=[smem, smem, vmem],
        out_specs=[vmem] * 4,
        out_shape=[step_shape]
        + [slab_shape] * 2
        + [jax.ShapeDtypeStruct((4, tiles, modes, 128), f32)],
        compiler_params=params(58),
        cost_estimate=cost(field_flops, 3 * field_bytes),
        name="factor",
    )(lower, upper, sigma)
    rings = [[(i, (i + n) % blocks) for i in range(blocks)] for n in range(1, blocks)]
    vw = jnp.stack([vw_ends] + [lax.ppermute(vw_ends, "gy", ring) for ring in rings])
    weight = jnp.broadcast_to((0.5 * width)[:, None], (rows, 128))
    end_gaps = jnp.stack([gaps[0], gaps[rows]])
    span_here, vw, weight, end_gaps = lax.optimization_barrier((span_here, vw, weight, end_gaps))

    flat = (span_length * modes, rows)
    hbm = pl.BlockSpec(memory_space=pltpu.HBM)
    span_source = pl.pallas_call(
        span_first_kernel,
        in_specs=[vmem, vmem],
        out_specs=vmem,
        out_shape=slab_shape,
        compiler_params=params(58),
        cost_estimate=cost(field_flops, 2 * field_bytes),
        name="span_first",
    )(span_here.reshape(flat), jnp.asarray(slots_right(span_derive)))
    slab = pltpu.VMEM(slab_shape.shape, f32)
    source, y_ends = pl.pallas_call(
        source_kernel,
        in_specs=[vmem, vmem, smem] + [hbm] * 4,
        out_specs=[vmem] * 2,
        out_shape=[slab_shape, jax.ShapeDtypeStruct((2, tiles, modes, 128), f32)],
        scratch_shapes=[
            pltpu.VMEM((2, 3 * span_length // 2, span_length // 2), bf16),
            slab,
            slab,
            slab,
            pltpu.SemaphoreType.DMA((13,)),
        ],
        compiler_params=params(48),
        cost_estimate=cost(field_flops, 5 * field_bytes),
        name="source",
    )(
        flow_here.reshape(flat),
        weight,
        end_gaps,
        jnp.asarray(slots_right(span_forward)),
        span_source,
        v_all,
        w_all,
    )
    ends = [y_ends] + [lax.ppermute(y_ends, "gy", ring) for ring in rings]
    step = pltpu.VMEM(step_shape.shape, f32)
    y_all = pl.pallas_call(
        sweep_kernel,
        in_specs=[smem, smem, vmem, hbm],
        out_specs=vmem,
        out_shape=slab_shape,
        scratch_shapes=[step] * 2 + [pltpu.SemaphoreType.DMA((4,))],
        compiler_params=params(32),
        cost_estimate=cost(field_flops, 3 * field_bytes),
        name="sweep",
    )(lower, upper, source, inv)
    end_shape = (blocks + 1, tiles, modes, 128)
    back_sent = pl.pallas_call(
        join_kernel,
        in_specs=[smem] + [vmem] * (2 + blocks) + [hbm] * 3,
        out_specs=vmem,
        out_shape=jax.ShapeDtypeStruct((group, modes, planes, rows), f32),
        scratch_shapes=[
            pltpu.VMEM((blocks, 2, tiles, modes, 128), f32),
            pltpu.VMEM(end_shape, f32),
            pltpu.VMEM(end_shape, f32),
            slab,
            slab,
            pltpu.VMEM((2, span_length // 2, 3 * span_length // 2), bf16),
            pltpu.SemaphoreType.DMA((9,)),
        ],
        compiler_params=params(32),
        cost_estimate=cost(field_flops, 4 * field_bytes),
        name="join",
    )(
        me.reshape(1).astype(jnp.int32),
        y_all,
        *ends,
        vw,
        v_all,
        w_all,
        jnp.asarray(nodes_left(span_inverse)),
    )
    back_here = moved(back_sent)
    last_table = jnp.asarray(nodes_left(flow_inverse))
    return pl.pallas_call(
        flow_inverse_kernel,
        in_specs=[vmem] * 2,
        out_specs=any_place,
        out_shape=jax.ShapeDtypeStruct((planes, flow_length, rows), f32),
        scratch_shapes=[
            pltpu.VMEM((planes, flow_length, rows), f32),
            pltpu.SemaphoreType.DMA((4,)),
        ],
        compiler_params=params(32),
        cost_estimate=cost(field_flops, 2 * field_bytes),
        name="flow_inverse",
    )(back_here.reshape(flow_length * planes, rows), last_table)


def solution(mesh):
    return jax.shard_map(
        local,
        mesh=mesh,
        in_specs=(P(None, ("gx", "gz"), None, "gy"), P()),
        out_specs=P(("gx", "gz"), None, "gy"),
        check_vma=False,
    )
```
